32 devices in a mesh: rep: 4 (over x, core), dp: 8 (over z, y).
Axes of the slice: x: 2, y: 2, z: 4, core: 2. Of those that a mesh axis runs over, the one named last changes fastest.
Arguments:
- features: float32 [288, 15, 15, 512], P(('rep', 'dp')), may hold values from -6 to 6
- map_size: int32 [288], P(('rep', 'dp')), may hold values from 13 to 15, as said below
- item_count: int32 [32], P(('rep', 'dp')), may hold values from 2 to 9, as said below
- conv4_weight: float32 [2359296], P(('rep', 'dp')), may hold values from -0.09375 to 0.09375
- conv4_bias: float32 [512], replicated, may hold values from -3 to 3
- conv5_weight: float32 [2359296], P(('rep', 'dp')), may hold values from -0.09375 to 0.09375
- conv5_bias: float32 [512], replicated, may hold values from -3 to 3
- cotangent: float32 [288, 15, 15, 512], P(('rep', 'dp')), may hold values from -6 to 6
Outputs:
- conv5_out: float32 [288, 15, 15, 512], P(('rep', 'dp'))
- input_grad: float32 [288, 15, 15, 512], P(('rep', 'dp'))
- conv4_weight_grad: float32 [2359296], P(('rep', 'dp'))
- conv4_bias_grad: float32 [512], replicated
- conv5_weight_grad: float32 [2359296], P(('rep', 'dp'))
- conv5_bias_grad: float32 [512], replicated
The draws below stay inside these ranges and needn't reach their ends.
Inputs may be any that keep to these rules, and one draw needn't show every extreme that they name: `map_size`: each item's map is 13 or 15 cells on a side, in the upper left corner of its slot; both sizes occur in every draw. `item_count`: the number of live items in each device's 9 slots, which come first; slots at or past it are empty; some device is full and some holds the fewest.
All inputs are finite; a program needn't handle non-finite values.
Results may differ from the reference program's by a relative error of at most 0.0003.
Values sent between devices are 32-bit elements; how exact they have to be, the bound alone decides.
No kernel may reach another device: no remote copies, remote signals or barrier semaphores. Data moves between devices by JAX's collectives and lax.ppermute only.
A program may use at most 384 MiB of HBM per device.

```python
import jax
import jax.numpy as jnp
from jax import lax

C = 512
SIDE = 15
SMALL_SIDE = 13
SLOTS = 9
DEVS = 32
ITEMS = 288


def draw_map_size(key, part):
    key = jax.random.fold_in(key, 11)
    coin_key, pick_key = jax.random.split(key)
    coins = jax.random.randint(coin_key, (ITEMS,), 0, 2)
    sizes = SMALL_SIDE + (SIDE - SMALL_SIDE) * coins
    order = jax.random.permutation(pick_key, ITEMS)
    sizes = sizes.at[order[0]].set(SIDE).at[order[1]].set(SMALL_SIDE)
    return sizes.astype(jnp.int32)


def draw_item_count(key, part):
    key = jax.random.fold_in(key, 23)
    count_key, pick_key = jax.random.split(key)
    fewest = max(1, SLOTS // 4)
    counts = jax.random.randint(count_key, (DEVS,), fewest, SLOTS + 1)
    order = jax.random.permutation(pick_key, DEVS)
    counts = counts.at[order[0]].set(SLOTS).at[order[1]].set(fewest)
    return counts.astype(jnp.int32)


def shard_levels(stream_key, shape, cuts, smallest, high):
    def one(axis_at, parts):
        steps = jax.random.uniform(jax.random.fold_in(jax.random.fold_in(stream_key, 6), axis_at), (parts,), jnp.float32, smallest / len(cuts), high / len(cuts))
        return jnp.repeat(jnp.exp(steps), shape[axis_at] // parts).reshape((-1,) + (1,) * (len(shape) - axis_at - 1))

    factor_of = one(*cuts[0])
    for cut in cuts[1:]:
        factor_of = factor_of * one(*cut)
    return factor_of


def centred(stream_key, shape, scale, most, shards=(), held_as=jnp.bfloat16):
    factor_of = shard_levels(stream_key, shape, shards, -0.22, 0.18) if shards else 1.0
    drawn = jax.random.normal(stream_key, shape, jnp.float32) * scale * factor_of
    return jnp.minimum(jnp.maximum(drawn, -most), most).astype(held_as)


def setup_inputs(seed: int = 0) -> dict:
    keys = jax.random.split(jax.random.key(seed), 9)
    features = centred(keys[0], (ITEMS, SIDE, SIDE, C), 1.0, 6.0, ((0, 32),), jnp.float32)
    map_size = draw_map_size(jax.random.fold_in(keys[8], 71), 0)
    item_count = draw_item_count(jax.random.fold_in(keys[8], 71), 0)
    conv4_weight = centred(keys[3], (9 * C * C,), (9 * C) ** -0.5, 0.09375, ((0, 32),), jnp.float32)
    conv4_bias = centred(keys[4], (C,), 0.5, 3.0, (), jnp.float32)
    conv5_weight = centred(keys[5], (9 * C * C,), (9 * C) ** -0.5, 0.09375, ((0, 32),), jnp.float32)
    conv5_bias = centred(keys[6], (C,), 0.5, 3.0, (), jnp.float32)
    cotangent = centred(keys[7], (ITEMS, SIDE, SIDE, C), 1.0, 6.0, ((0, 32),), jnp.float32)
    return dict(features=features, map_size=map_size, item_count=item_count, conv4_weight=conv4_weight, conv4_bias=conv4_bias, conv5_weight=conv5_weight, conv5_bias=conv5_bias, cotangent=cotangent)


@jax.custom_vjp
def low(v):
    return lax.optimization_barrier(v.astype(jnp.bfloat16)).astype(jnp.float32)

@jax.custom_vjp
def low_back(v):
    return v

def low_keep(v):
    return (low(v), None)

def low_pass(kept, grad):
    return (grad,)

def back_keep(v):
    return (v, None)

def back_low(kept, grad):
    return (low(grad),)
low.defvjp(low_keep, low_pass)
low_back.defvjp(back_keep, back_low)

def smooth_act(values):
    return jax.nn.gelu(values, approximate=True)

def convolve(source, kernel, offset):
    padded = jnp.pad(source, ((0, 0), (1, 1), (1, 1), (0, 0)))
    summed = jnp.zeros(source.shape, jnp.float32) + offset
    for row_tap in range(3):
        for col_tap in range(3):
            window = padded[:, row_tap:row_tap + SIDE, col_tap:col_tap + SIDE, :]
            summed = summed + jnp.einsum('iyxc,cd->iyxd', window, kernel[row_tap, col_tap], precision=lax.Precision.HIGHEST)
    return summed

def reference(features, map_size, item_count, conv4_weight, conv4_bias, conv5_weight, conv5_bias, cotangent):
    item_ids = jnp.arange(ITEMS, dtype=jnp.int32)
    live = item_ids % SLOTS < jnp.repeat(item_count, SLOTS)
    cells = jnp.arange(SIDE, dtype=jnp.int32)
    inside = cells[None, :] < map_size[:, None]
    valid = live[:, None, None] & inside[:, :, None] & inside[:, None, :]
    valid_mask = valid.astype(jnp.float32)[..., None]

    def forward(source, kernel4, offset4, kernel5, offset5):
        masked = source * valid_mask
        hidden = smooth_act(convolve(masked, kernel4, offset4)) * valid_mask
        return smooth_act(convolve(hidden, kernel5, offset5)) * valid_mask
    conv5_out, pullback = jax.vjp(forward, features, conv4_weight.reshape(3, 3, C, C), conv4_bias, conv5_weight.reshape(3, 3, C, C), conv5_bias)
    grad_input, grad_k4, grad_b4, grad_k5, grad_b5 = pullback(cotangent)
    grad_scale = float(ITEMS * SIDE * SIDE) ** (-0.5)
    return (conv5_out, grad_input, grad_k4.reshape(-1) * grad_scale, grad_b4 * grad_scale, grad_k5.reshape(-1) * grad_scale, grad_b5 * grad_scale)
```

```python
import functools

import jax
import jax.numpy as jnp
from jax import lax
from jax.experimental import pallas as pl
from jax.experimental.pallas import tpu as pltpu
from jax.sharding import PartitionSpec as P

AXES = ("rep", "dp")
F32 = jnp.float32
BF16 = jnp.bfloat16
LANES = 128
VMEM_LIMIT = 62 * 2**20
NN = (((1,), (0,)), ((), ()))
NT = (((1,), (1,)), ((), ()))
TN = (((0,), (0,)), ((), ()))
GELU_K = 0.7978845608028654
GELU_C = 0.044715


def patch_to_points(p0, p1, p2, p3, p4):
    d31 = p3 - p1
    return (
        2.0 * (p0 - p2) + d31,
        (p3 - p2) - 2.0 * p1,
        2.0 * p1 - 3.0 * p2 + p3,
        d31,
        (p4 - p2) - 2.0 * d31,
    )


def points_to_patch(n0, n1, n2, n3, n4):
    s = n1 + n2
    return (
        2.0 * (n2 - n1 + n4) - (n0 + n3),
        -(2.0 * (n0 + n2) + (s + n4)),
        (n0 + s) + (n3 - 2.0 * n4),
    )


def taps_to_points(k0, k1, k2):
    s = k0 + k2
    return (k0, s + k1, s - k1, k0 + 2.0 * (k1 + 2.0 * k2), k2)


def taps_to_point(index, k0, k1, k2):
    if index == 0:
        return k0
    if index == 1:
        return (k0 + k2) + k1
    if index == 2:
        return (k0 + k2) - k1
    if index == 3:
        return k0 + 2.0 * (k1 + 2.0 * k2)
    return k2


POINT_TAPS = (((0, 1.0),), ((0, 1.0), (1, 1.0), (2, 1.0)), ((0, 1.0), (1, -1.0), (2, 1.0)), ((0, 1.0), (1, 2.0), (2, 4.0)), ((2, 1.0),))


def points_to_taps(d0, d1, d2, d3, d4):
    s = d1 + d2
    return (d0 + s + d3, (d1 - d2) + 2.0 * d3, s + 4.0 * d3 + d4)


def points_to_cells(m0, m1, m2, m3, m4):
    half = 0.5 * m1
    f = (1.0 / 6.0) * m2
    g = (1.0 / 6.0) * m3
    return (0.5 * m0 - half - f + g, f - half + 2.0 * g, (4.0 * g - half) + (m4 - f))


def cells_to_points(y0, y1, y2):
    s = y0 + y2
    return (
        0.5 * y0,
        -0.5 * (s + y1),
        (1.0 / 6.0) * (y1 - s),
        (1.0 / 6.0) * (y0 + 2.0 * (y1 + 2.0 * y2)),
        y2,
    )


def split(value):
    high = value.astype(BF16)
    return high, (value - high.astype(F32)).astype(BF16)


def dot3(left_high, left_low, right_high, right_low, dims):
    def dot(left, right):
        return lax.dot_general(left, right, dims, preferred_element_type=F32)

    return dot(left_high, right_high) + dot(left_low, right_high) + dot(left_high, right_low)


def gelu_parts(v):
    square = v * v
    t = jnp.tanh(GELU_K * (v + GELU_C * (square * v)))
    half = 0.5 * (1.0 + t)
    slope = half + (0.5 * v) * (1.0 - t * t) * (GELU_K + (3.0 * GELU_K * GELU_C) * square)
    return v * half, slope


def segments(tap, start, rows, tap_rows, block_rows):
    cuts = []
    at = tap * tap_rows + start
    end = at + rows
    first = at
    while at < end:
        block = at // block_rows
        stop = min(end, (block + 1) * block_rows)
        cuts.append((block, at - block * block_rows, at - first, stop - at))
        at = stop
    return cuts


class Plan:
    def __init__(self, channels, rows, tiles, block_rows, n_pieces, n_outs):
        self.C = channels
        self.R = rows
        self.T = tiles
        self.block_rows = block_rows
        self.n_pieces = n_pieces
        self.n_outs = n_outs
        self.N = min(256, channels)


def for_each_cut(plan, tab, row, count, cut_block, act):
    if count == 1:
        act(0, 0)
        return
    which = tab[row, cut_block]
    index = tab[row + 1, cut_block]
    for ref in range(count):
        pl.when(which == ref)(functools.partial(act, ref, index))


def start_kernel_fetch(plan, tab, pieces, buf, sem, row_start, rows, col_start, cols):
    for tap in range(9):
        for block, at, to, length in segments(tap, row_start, rows, plan.C, plan.block_rows):

            def act(ref, index, tap=tap, at=at, to=to, length=length):
                pltpu.make_async_copy(
                    pieces[ref].at[index, pl.ds(at, length), pl.ds(col_start, cols)],
                    buf.at[tap, pl.ds(to, length)],
                    sem,
                ).start()

            for_each_cut(plan, tab, 0, plan.n_pieces, block, act)


def start_grad_store(plan, tab, buf, outs, sem, col_start, cols):
    for tap in range(9):
        for block, at, to, length in segments(tap, 0, plan.C, plan.C, plan.block_rows):

            def act(ref, index, tap=tap, at=at, to=to, length=length):
                pltpu.make_async_copy(
                    buf.at[tap, pl.ds(to, length)],
                    outs[ref].at[index, pl.ds(at, length), pl.ds(col_start, cols)],
                    sem,
                ).start()

            for_each_cut(plan, tab, 2, plan.n_outs, block, act)


def wait_for(buf, sem):
    pltpu.make_async_copy(buf, buf, sem).wait()


def edge_masks(plan):
    place = lax.broadcasted_iota(jnp.int32, (plan.R, LANES), 0) % plan.T
    return (place != 0).astype(F32), (place != plan.T - 1).astype(F32)


def make_patch_points(plan, x_hbm, xp, vh, vl, sem):
    T, R = plan.T, plan.R
    cols = 3 * T
    not_first, not_last = edge_masks(plan)
    chunks = plan.C // LANES

    def copy(chunk):
        slot = chunk % 2
        return pltpu.make_async_copy(
            x_hbm.at[:, :, :, pl.ds(chunk * LANES, LANES)],
            xp.at[slot, pl.ds(1, 3), pl.ds(1, cols)],
            sem.at[slot],
        )

    for slot in range(2):
        for plane in range(5):
            for col in (0, cols + 1):
                xp[slot, plane, col] = jnp.zeros((R, LANES), F32)
    copy(0).start()
    for chunk in range(chunks):
        slot = chunk % 2
        copy(chunk).wait()
        if chunk + 1 < chunks:
            copy(chunk + 1).start()

        def shift(col, _, slot=slot):
            xp[slot, 0, col + 1] = pltpu.roll(xp[slot, 3, col + 1], 1, 0) * not_first
            xp[slot, 4, col + 1] = pltpu.roll(xp[slot, 1, col + 1], R - 1, 0) * not_last
            return 0

        lax.fori_loop(0, cols, shift, 0)

        def body(j, _, slot=slot, chunk=chunk):
            for rb in range(0, R, 16):
                points = []
                for v in range(5):
                    patch = [xp[slot, u, 3 * j + v, pl.ds(rb, 16)] for u in range(5)]
                    points.append(patch_to_points(*patch))
                for u in range(5):
                    row = patch_to_points(*[points[v][u] for v in range(5)])
                    for v in range(5):
                        high, low = split(row[v])
                        vh[u, v, j, pl.ds(rb, 16), pl.ds(chunk * LANES, LANES)] = high
                        vl[u, v, j, pl.ds(rb, 16), pl.ds(chunk * LANES, LANES)] = low
            return 0

        lax.fori_loop(0, T, body, 0)


def make_cell_points(plan, y_hbm, yb, wh, wl, sem, first_chunk, chunks):
    T, R = plan.T, plan.R

    def copy(chunk):
        slot = chunk % 2
        return pltpu.make_async_copy(
            y_hbm.at[:, :, :, pl.ds((first_chunk + chunk) * LANES, LANES)], yb.at[slot], sem.at[slot]
        )

    copy(0).start()
    for chunk in range(chunks):
        slot = chunk % 2
        copy(chunk).wait()
        if chunk + 1 < chunks:
            copy(chunk + 1).start()

        def body(j, _, slot=slot, chunk=chunk):
            for rb in range(0, R, 16):
                points = []
                for b in range(3):
                    cells = [yb[slot, a, 3 * j + b, pl.ds(rb, 16)] for a in range(3)]
                    points.append(cells_to_points(*cells))
                for u in range(5):
                    row = cells_to_points(*[points[b][u] for b in range(3)])
                    for v in range(5):
                        high, low = split(row[v])
                        wh[u, v, j, pl.ds(rb, 16), pl.ds(chunk * LANES, LANES)] = high
                        wl[u, v, j, pl.ds(rb, 16), pl.ds(chunk * LANES, LANES)] = low
            return 0

        lax.fori_loop(0, T, body, 0)


def make_tap_points(kbuf, uh, ul, point):
    rows = kbuf.shape[1]
    step = 16

    def body(i, _):
        at = pl.ds(pl.multiple_of(i * step, step), step)
        parts = [taps_to_point(point, kbuf[q, at], kbuf[3 + q, at], kbuf[6 + q, at]) for q in range(3)]
        for v, value in enumerate(taps_to_points(*parts)):
            high, low = split(value)
            uh[v, at] = high
            ul[v, at] = low
        return 0

    lax.fori_loop(0, rows // step, body, 0)


def forward_kernel(plan, last, tab, mask, bias, *refs):
    refs = list(refs)
    C, N, R, T = plan.C, plan.N, plan.R, plan.T
    cols = 3 * T
    x_hbm = refs.pop(0)
    cot_hbm = refs.pop(0) if last else None
    pieces = [refs.pop(0) for _ in range(plan.n_pieces)]
    act_hbm, slope_hbm = refs.pop(0), refs.pop(0)
    bias_sum = refs.pop(0) if last else None
    xp, vh, vl, kbuf, uh, ul, mbuf, ebuf, stage, x_sem, k_sem, out_sem = refs[:12]
    cbuf, c_sem = refs[12:] if last else (None, None)
    chunks = C // N
    for n in range(chunks):
        start_kernel_fetch(plan, tab, pieces, kbuf.at[n], k_sem.at[n], 0, C, n * N, N)
    if last:
        for n in range(chunks):
            pltpu.make_async_copy(cot_hbm.at[:, :, :, pl.ds(n * N, N)], cbuf.at[n], c_sem.at[n]).start()
    make_patch_points(plan, x_hbm, xp, vh, vl, x_sem)
    for n in range(chunks):
        wait_for(kbuf.at[n], k_sem.at[n])
        for u in range(5):
            make_tap_points(kbuf.at[n], uh, ul, u)
            for v in range(5):
                left = (vh[u, v].reshape(T * R, C), vl[u, v].reshape(T * R, C))
                mbuf[v] = dot3(*left, uh[v], ul[v], NN).reshape(T, R, N)

            def columns(j, _, u=u):
                for rb in range(0, R, 16):
                    cells = points_to_cells(*[mbuf[v, j, pl.ds(rb, 16)] for v in range(5)])
                    for b in range(3):
                        ebuf[u, 3 * j + b, pl.ds(rb, 16)] = cells[b]
                return 0

            lax.fori_loop(0, T, columns, 0)
        if last:
            pltpu.make_async_copy(cot_hbm.at[:, :, :, pl.ds(n * N, N)], cbuf.at[n], c_sem.at[n]).wait()
            stage[n, 2, 0, 0] = jnp.zeros((R, N), F32)

        def finish(col, _, n=n):
            for lane in range(0, N, LANES):
                at = pl.ds(lane, LANES)
                offset = bias[0:1, pl.ds(n * N + lane, LANES)]
                for rb in range(0, R, 16):
                    rows = pl.ds(rb, 16)
                    cells = points_to_cells(*[ebuf[u, col, rows, at] for u in range(5)])
                    for a in range(3):
                        value, slope = gelu_parts(cells[a] + offset)
                        keep = mask[a, col, rows]
                        stage[n, 0, a, col, rows, at] = value * keep
                        if last:
                            back = slope * keep * cbuf[n, a, col, rows, at]
                            stage[n, 1, a, col, rows, at] = back
                            stage[n, 2, 0, 0, rows, at] += back
                        else:
                            stage[n, 1, a, col, rows, at] = slope * keep
            return 0

        lax.fori_loop(0, cols, finish, 0)
        if last:
            bias_sum[0:1, pl.ds(n * N, N)] = jnp.sum(stage[n, 2, 0, 0], axis=0, keepdims=True)
        for which, out in ((0, act_hbm), (1, slope_hbm)):
            pltpu.make_async_copy(stage.at[n, which], out.at[:, :, :, pl.ds(n * N, N)], out_sem.at[which, n]).start()
    for n in range(chunks):
        for which, out in ((0, act_hbm), (1, slope_hbm)):
            pltpu.make_async_copy(stage.at[n, which], out.at[:, :, :, pl.ds(n * N, N)], out_sem.at[which, n]).wait()


def back_kernel(plan, last, tab, mask, y_hbm, *refs):
    refs = list(refs)
    C, N, R, T = plan.C, plan.N, plan.R, plan.T
    cols = 3 * T
    slope_hbm = None if last else refs.pop(0)
    pieces = [refs.pop(0) for _ in range(plan.n_pieces)]
    out_hbm = refs.pop(0)
    bias_sum = None if last else refs.pop(0)
    yb, wh, wl, kbuf, uh, ul, mbuf, ebuf, stage, y_sem, k_sem, out_sem = refs[:12]
    sbuf, total, s_sem = (None, None, None) if last else refs[12:]
    chunks = C // N
    for n in range(chunks):
        start_kernel_fetch(plan, tab, pieces, kbuf.at[n], k_sem.at[n], n * N, N, 0, C)
    if not last:
        for n in range(chunks):
            pltpu.make_async_copy(slope_hbm.at[:, :, :, pl.ds(n * N, N)], sbuf.at[n], s_sem.at[n]).start()
    make_cell_points(plan, y_hbm, yb, wh, wl, y_sem, 0, C // LANES)
    not_first, not_last = edge_masks(plan)
    for v in range(5):
        mbuf[v, 0] = jnp.zeros((R, N), F32)
        mbuf[v, T + 1] = jnp.zeros((R, N), F32)
    for n in range(chunks):
        wait_for(kbuf.at[n], k_sem.at[n])
        for u in range(5):
            make_tap_points(kbuf.at[n], uh, ul, u)
            for v in range(5):
                left = (wh[u, v].reshape(T * R, C), wl[u, v].reshape(T * R, C))
                mbuf[v, pl.ds(1, T)] = dot3(*left, uh[v], ul[v], NT).reshape(T, R, N)

            def columns(j, _, u=u):
                for rb in range(0, R, 16):
                    rows = pl.ds(rb, 16)
                    here = points_to_patch(*[mbuf[v, j + 1, rows] for v in range(5)])
                    ebuf[u, 3 * j, rows] = here[0] + mbuf[4, j, rows]
                    ebuf[u, 3 * j + 1, rows] = here[1]
                    ebuf[u, 3 * j + 2, rows] = here[2] + 2.0 * mbuf[0, j + 2, rows]
                return 0

            lax.fori_loop(0, T, columns, 0)
        if not last:
            pltpu.make_async_copy(slope_hbm.at[:, :, :, pl.ds(n * N, N)], sbuf.at[n], s_sem.at[n]).wait()
            total[...] = jnp.zeros((R, N), F32)

        def finish(col, _, n=n):
            for lane in range(0, N, LANES):
                at = pl.ds(lane, LANES)
                points = [ebuf[u, col, :, at] for u in range(5)]
                here = points_to_patch(*points)
                cells = (
                    here[0] + pltpu.roll(points[4], 1, 0) * not_first,
                    here[1],
                    here[2] + 2.0 * (pltpu.roll(points[0], R - 1, 0) * not_last),
                )
                for a in range(3):
                    if last:
                        stage[n, a, col, :, at] = cells[a] * mask[a, col]
                    else:
                        back = cells[a] * sbuf[n, a, col, :, at]
                        stage[n, a, col, :, at] = back
                        total[:, at] += back
            return 0

        lax.fori_loop(0, cols, finish, 0)
        if not last:
            bias_sum[0:1, pl.ds(n * N, N)] = jnp.sum(total[...], axis=0, keepdims=True)
        pltpu.make_async_copy(stage.at[n], out_hbm.at[:, :, :, pl.ds(n * N, N)], out_sem.at[n]).start()
    for n in range(chunks):
        pltpu.make_async_copy(stage.at[n], out_hbm.at[:, :, :, pl.ds(n * N, N)], out_sem.at[n]).wait()


def grad_kernel(plan, tab, x_hbm, y_hbm, *refs):
    refs = list(refs)
    C, N, R, T = plan.C, plan.N, plan.R, plan.T
    outs = [refs.pop(0) for _ in range(plan.n_outs)]
    xp, vh, vl, yb, wh, wl, dbuf, kgrad, x_sem, y_sem, out_sem = refs
    chunks = C // N
    step = 16
    make_patch_points(plan, x_hbm, xp, vh, vl, x_sem)
    for n in range(chunks):
        make_cell_points(plan, y_hbm, yb, wh, wl, y_sem, n * N // LANES, N // LANES)
        for u in range(5):
            for v in range(5):
                left = (vh[u, v].reshape(T * R, C), vl[u, v].reshape(T * R, C))
                right = (wh[u, v].reshape(T * R, N), wl[u, v].reshape(T * R, N))
                dbuf[v] = dot3(*left, *right, TN)

            def add(i, _, n=n, u=u):
                at = pl.ds(pl.multiple_of(i * step, step), step)
                taps = points_to_taps(*[dbuf[v, at] for v in range(5)])
                for p, weight in POINT_TAPS[u]:
                    for q in range(3):
                        term = taps[q] if weight == 1.0 else weight * taps[q]
                        if u == 0 or (u == 1 and p > 0):
                            kgrad[n, 3 * p + q, at] = term
                        else:
                            kgrad[n, 3 * p + q, at] += term
                return 0

            lax.fori_loop(0, C // step, add, 0)
        start_grad_store(plan, tab, kgrad.at[n], outs, out_sem.at[n], n * N, N)
    for n in range(chunks):
        wait_for(kgrad.at[n], out_sem.at[n])


SMEM_SPEC = pl.BlockSpec(memory_space=pltpu.SMEM)
VMEM_SPEC = pl.BlockSpec(memory_space=pltpu.VMEM)
ANY_SPEC = pl.BlockSpec(memory_space=pl.ANY)


def plane_shape(plan):
    return jax.ShapeDtypeStruct((3, 3 * plan.T, plan.R, plan.C), F32)


def point_scratch(plan, width):
    shape = (5, 5, plan.T, plan.R, width)
    return [pltpu.VMEM(shape, BF16), pltpu.VMEM(shape, BF16)]


def call(kernel, outs, in_specs, out_specs, scratch, flops, args, name):
    moved = sum(a.size * a.dtype.itemsize for a in args) + sum(o.size * 4 for o in outs)
    return pl.pallas_call(
        kernel,
        out_shape=outs,
        in_specs=in_specs,
        out_specs=out_specs,
        scratch_shapes=scratch,
        compiler_params=pltpu.CompilerParams(vmem_limit_bytes=VMEM_LIMIT),
        cost_estimate=pl.CostEstimate(flops=flops, bytes_accessed=moved, transcendentals=0),
        name=name,
    )(*args)


def pass_flops(plan):
    return 2 * 3 * 25 * plan.T * plan.R * plan.C * plan.C


def run_forward(plan, tab, mask, bias, x, cot, pieces, name):
    last = cot is not None
    C, N, R, T = plan.C, plan.N, plan.R, plan.T
    cols = 3 * T
    chunks = C // N
    outs = [plane_shape(plan), plane_shape(plan)]
    out_specs = [ANY_SPEC, ANY_SPEC]
    scratch = [
        pltpu.VMEM((2, 5, cols + 2, R, LANES), F32),
        *point_scratch(plan, C),
        pltpu.VMEM((chunks, 9, C, N), F32),
        pltpu.VMEM((5, C, N), BF16),
        pltpu.VMEM((5, C, N), BF16),
        pltpu.VMEM((5, T, R, N), F32),
        pltpu.VMEM((5, cols, R, N), F32),
        pltpu.VMEM((chunks, 2 + last, 3, cols, R, N), F32) if not last else pltpu.VMEM((chunks, 3, 3, cols, R, N), F32),
        pltpu.SemaphoreType.DMA((2,)),
        pltpu.SemaphoreType.DMA((chunks,)),
        pltpu.SemaphoreType.DMA((2, chunks)),
    ]
    args = [tab, mask, bias, x]
    if last:
        outs.append(jax.ShapeDtypeStruct((1, C), F32))
        out_specs.append(VMEM_SPEC)
        scratch += [pltpu.VMEM((chunks, 3, cols, R, N), F32), pltpu.SemaphoreType.DMA((chunks,))]
        args.append(cot)
    args += pieces
    in_specs = [SMEM_SPEC, VMEM_SPEC, VMEM_SPEC] + [ANY_SPEC] * (len(args) - 3)
    kernel = functools.partial(forward_kernel, plan, last)
    return call(kernel, outs, in_specs, out_specs, scratch, pass_flops(plan), args, name)


def run_back(plan, tab, mask, y, slope, pieces, name):
    last = slope is None
    C, N, R, T = plan.C, plan.N, plan.R, plan.T
    cols = 3 * T
    chunks = C // N
    outs = [plane_shape(plan)]
    out_specs = [ANY_SPEC]
    scratch = [
        pltpu.VMEM((2, 3, cols, R, LANES), F32),
        *point_scratch(plan, C),
        pltpu.VMEM((chunks, 9, N, C), F32),
        pltpu.VMEM((5, N, C), BF16),
        pltpu.VMEM((5, N, C), BF16),
        pltpu.VMEM((5, T + 2, R, N), F32),
        pltpu.VMEM((5, cols, R, N), F32),
        pltpu.VMEM((chunks, 3, cols, R, N), F32),
        pltpu.SemaphoreType.DMA((2,)),
        pltpu.SemaphoreType.DMA((chunks,)),
        pltpu.SemaphoreType.DMA((chunks,)),
    ]
    args = [tab, mask, y]
    if not last:
        outs.append(jax.ShapeDtypeStruct((1, C), F32))
        out_specs.append(VMEM_SPEC)
        scratch += [
            pltpu.VMEM((chunks, 3, cols, R, N), F32),
            pltpu.VMEM((R, N), F32),
            pltpu.SemaphoreType.DMA((chunks,)),
        ]
        args.append(slope)
    args += pieces
    in_specs = [SMEM_SPEC, VMEM_SPEC] + [ANY_SPEC] * (len(args) - 2)
    kernel = functools.partial(back_kernel, plan, last)
    return call(kernel, outs, in_specs, out_specs, scratch, pass_flops(plan), args, name)


def run_grad(plan, tab, x, y, name):
    C, N, R, T = plan.C, plan.N, plan.R, plan.T
    cols = 3 * T
    chunks = C // N
    blocks = 9 * C // plan.block_rows // plan.n_outs
    outs = [jax.ShapeDtypeStruct((blocks, plan.block_rows, C), F32) for _ in range(plan.n_outs)]
    scratch = [
        pltpu.VMEM((2, 5, cols + 2, R, LANES), F32),
        *point_scratch(plan, C),
        pltpu.VMEM((2, 3, cols, R, LANES), F32),
        *point_scratch(plan, N),
        pltpu.VMEM((5, C, N), F32),
        pltpu.VMEM((chunks, 9, C, N), F32),
        pltpu.SemaphoreType.DMA((2,)),
        pltpu.SemaphoreType.DMA((2,)),
        pltpu.SemaphoreType.DMA((chunks,)),
    ]
    in_specs = [SMEM_SPEC, ANY_SPEC, ANY_SPEC]
    kernel = functools.partial(grad_kernel, plan)
    return call(kernel, outs, in_specs, [ANY_SPEC] * plan.n_outs, scratch, pass_flops(plan), [tab, x, y], name)


def to_planes(plan, cells):
    slots, side, _, channels = cells.shape
    tiled = cells.reshape(slots, plan.T, 3, side, channels).transpose(2, 3, 0, 1, 4)
    flat = tiled.reshape(3, side, slots * plan.T, channels)
    return jnp.pad(flat, ((0, 0), (0, 0), (0, plan.R - slots * plan.T), (0, 0)))


def from_planes(plan, planes, slots):
    side = 3 * plan.T
    kept = planes[:, :, : slots * plan.T].reshape(3, side, slots, plan.T, planes.shape[3])
    return kept.transpose(2, 3, 0, 1, 4).reshape(slots, side, side, planes.shape[3])


class Net:
    def __init__(self):
        self.rep = lax.axis_size("rep")
        self.dp = lax.axis_size("dp")
        self.routed = self.rep == 4 and self.dp == 8
        self.n_pieces = 4 if self.routed else 1
        self.n_outs = 2 if self.routed else 1

    def perm(self, move):
        pairs = []
        for x in range(2):
            for c in range(2):
                for z in range(4):
                    for y in range(2):
                        to = move(x, c, z, y)
                        pairs.append((((x * 2 + c) * 4 + z) * 2 + y, ((to[0] * 2 + to[1]) * 4 + to[2]) * 2 + to[3]))
        return pairs

    def send(self, value, move):
        return lax.ppermute(value, AXES, self.perm(move))

    def over_core(self, value):
        return self.send(value, lambda x, c, z, y: (x, 1 - c, z, y))

    def over_first(self, value):
        return self.send(value, lambda x, c, z, y: (x, c, z, 1 - y) if c == 0 else (1 - x, c, z, y))

    def over_second(self, value):
        return self.send(value, lambda x, c, z, y: (1 - x, c, z, y) if c == 0 else (x, c, z, 1 - y))

    def over_z(self, value, step):
        return self.send(value, lambda x, c, z, y: (x, c, (z + step) % 4, y))

    def tables(self):
        if not self.routed:
            return jnp.zeros((4, 8), jnp.int32)
        rep = lax.axis_index("rep")
        dp = lax.axis_index("dp")
        x, c, z, y = rep // 2, rep % 2, dp // 2, dp % 2
        block = jnp.arange(32, dtype=jnp.int32)
        bx, bc, bz, by = block // 16, block // 8 % 2, block // 2 % 4, block % 2
        dx, dy = bx ^ x, by ^ y
        second = jnp.where(bc == 0, dx, dy)
        first = jnp.where(bc == 0, dy, dx)
        other = (bc != c).astype(jnp.int32)
        return jnp.stack(
            [2 * other + second, 4 * first + (z - bz) % 4, other, 8 * second + 4 * first + (bz - z) % 4]
        ).astype(jnp.int32)

    def gather(self, shard):
        if not self.routed:
            return [lax.all_gather(shard, AXES, axis=0, tiled=True)[None]]
        four = jnp.stack([shard] + [self.over_z(shard, step) for step in (1, 2, 3)])
        eight = jnp.concatenate([four, self.over_first(four)])
        far = self.over_second(eight)
        return [eight, far, self.over_core(eight), self.over_core(far)]

    def scatter_sum(self, parts):
        if not self.routed:
            return lax.psum_scatter(parts[0][0], AXES, scatter_dimension=0, tiled=True)
        mine, theirs = parts
        got = self.over_core(theirs)
        got = self.over_second(mine[8:] + got[8:]) + (mine[:8] + got[:8])
        got = self.over_first(got[4:]) + got[:4]
        total = got[0]
        for step in (1, 2, 3):
            total = total + self.over_z(got[step], step)
        return total

    def total(self, value):
        if not self.routed:
            return lax.psum(value, AXES)
        value = value + self.over_core(value)
        value = value + self.over_second(value)
        value = value + self.over_first(value)
        return value + self.over_z(value, 1) + self.over_z(value, 2) + self.over_z(value, 3)


def body(
    features, map_size, item_count, conv4_weight, conv4_bias, conv5_weight, conv5_bias, cotangent
):
    slots, side, _, channels = features.shape
    net = Net()
    tiles = side // 3
    rows = -(-slots * tiles // 16) * 16
    shard_rows = conv4_weight.shape[0] // channels
    block_rows = shard_rows if net.routed else 9 * channels
    plan = Plan(channels, rows, tiles, block_rows, net.n_pieces, net.n_outs)

    live = jnp.arange(slots, dtype=jnp.int32) < item_count[0]
    inside = jnp.arange(side, dtype=jnp.int32)[None, :] < map_size[:, None]
    valid = live[:, None, None] & inside[:, :, None] & inside[:, None, :]
    mask = to_planes(plan, jnp.broadcast_to(valid.astype(F32)[..., None], (slots, side, side, LANES)))
    source = to_planes(plan, features * valid.astype(F32)[..., None])
    cot = to_planes(plan, cotangent)
    tab = net.tables()

    pieces4 = net.gather(conv4_weight.reshape(shard_rows, channels))
    pieces5 = net.gather(conv5_weight.reshape(shard_rows, channels))
    hidden, slope4 = run_forward(plan, tab, mask, conv4_bias[None], source, None, pieces4, "conv4")
    out5, back5, bias5 = run_forward(plan, tab, mask, conv5_bias[None], hidden, cot, pieces5, "conv5")
    grad5 = run_grad(plan, tab, hidden, back5, "grad5")
    back4, bias4 = run_back(plan, tab, mask, back5, slope4, pieces5, "back5")
    grad4 = run_grad(plan, tab, source, back4, "grad4")
    input_grad = run_back(plan, tab, mask, back4, None, pieces4, "back4")[0]

    total_cells = slots * net.rep * net.dp * side * side
    scale = float(total_cells) ** (-0.5)
    share5 = net.scatter_sum(grad5)
    share4 = net.scatter_sum(grad4)
    biases = net.total(jnp.concatenate([bias4, bias5])) * scale
    return (
        from_planes(plan, out5, slots),
        from_planes(plan, input_grad, slots),
        (share4 * scale).reshape(-1),
        biases[0],
        (share5 * scale).reshape(-1),
        biases[1],
    )


def solution(mesh):
    placed = (
        P(AXES, None, None, None),
        P(AXES),
        P(AXES),
        P(AXES),
        P(),
        P(AXES),
        P(),
        P(AXES, None, None, None),
    )
    return jax.shard_map(
        body,
        mesh=mesh,
        in_specs=placed,
        out_specs=(
            P(AXES, None, None, None),
            P(AXES, None, None, None),
            P(AXES),
            P(),
            P(AXES),
            P(),
        ),
        check_vma=False,
    )
```

```python
import functools

import jax
import jax.numpy as jnp
from jax import lax
from jax.experimental import pallas as pl
from jax.experimental.pallas import tpu as pltpu
from jax.sharding import PartitionSpec as P

AXES = ("rep", "dp")
F32 = jnp.float32
BF16 = jnp.bfloat16
LANES = 128
VMEM_LIMIT = 62 * 2**20
NN = (((1,), (0,)), ((), ()))
NT = (((1,), (1,)), ((), ()))
TN = (((0,), (0,)), ((), ()))
GELU_K = 0.7978845608028654
GELU_C = 0.044715


def patch_to_points(p0, p1, p2, p3, p4):
    d31 = p3 - p1
    return (
        2.0 * (p0 - p2) + d31,
        (p3 - p2) - 2.0 * p1,
        2.0 * p1 - 3.0 * p2 + p3,
        d31,
        (p4 - p2) - 2.0 * d31,
    )


def points_to_patch(n0, n1, n2, n3, n4):
    s = n1 + n2
    return (
        2.0 * (n2 - n1 + n4) - (n0 + n3),
        -(2.0 * (n0 + n2) + (s + n4)),
        (n0 + s) + (n3 - 2.0 * n4),
    )


def taps_to_points(k0, k1, k2):
    s = k0 + k2
    return (k0, s + k1, s - k1, k0 + 2.0 * (k1 + 2.0 * k2), k2)


def taps_to_point(index, k0, k1, k2, at):
    if index == 0:
        return k0[at]
    if index == 1:
        return (k0[at] + k2[at]) + k1[at]
    if index == 2:
        return (k0[at] + k2[at]) - k1[at]
    if index == 3:
        return k0[at] + 2.0 * (k1[at] + 2.0 * k2[at])
    return k2[at]


POINT_TAPS = (((0, 1.0),), ((0, 1.0), (1, 1.0), (2, 1.0)), ((0, 1.0), (1, -1.0), (2, 1.0)), ((0, 1.0), (1, 2.0), (2, 4.0)), ((2, 1.0),))


def points_to_taps(d0, d1, d2, d3, d4):
    s = d1 + d2
    return (d0 + s + d3, (d1 - d2) + 2.0 * d3, s + 4.0 * d3 + d4)


def points_to_cells(m0, m1, m2, m3, m4):
    half = 0.5 * m1
    f = (1.0 / 6.0) * m2
    g = (1.0 / 6.0) * m3
    return (0.5 * m0 - half - f + g, f - half + 2.0 * g, (4.0 * g - half) + (m4 - f))


def cells_to_points(y0, y1, y2):
    s = y0 + y2
    return (
        0.5 * y0,
        -0.5 * (s + y1),
        (1.0 / 6.0) * (y1 - s),
        (1.0 / 6.0) * (y0 + 2.0 * (y1 + 2.0 * y2)),
        y2,
    )


def split(value):
    high = value.astype(BF16)
    return high, (value - high.astype(F32)).astype(BF16)


def dot3(left_high, left_low, right_high, right_low, dims):
    def dot(left, right):
        return lax.dot_general(left, right, dims, preferred_element_type=F32)

    return dot(left_high, right_high) + dot(left_low, right_high) + dot(left_high, right_low)


def gelu_parts(v):
    square = v * v
    t = jnp.tanh(GELU_K * (v + GELU_C * (square * v)))
    half = 0.5 * (1.0 + t)
    slope = half + (0.5 * v) * (1.0 - t * t) * (GELU_K + (3.0 * GELU_K * GELU_C) * square)
    return v * half, slope


def segments(tap, start, rows, tap_rows, block_rows):
    cuts = []
    at = tap * tap_rows + start
    end = at + rows
    first = at
    while at < end:
        block = at // block_rows
        stop = min(end, (block + 1) * block_rows)
        cuts.append((block, at - block * block_rows, at - first, stop - at))
        at = stop
    return cuts


class Plan:
    def __init__(self, channels, rows, tiles, block_rows, n_pieces, n_outs):
        self.C = channels
        self.R = rows
        self.T = tiles
        self.block_rows = block_rows
        self.n_pieces = n_pieces
        self.n_outs = n_outs
        self.N = min(256, channels)


def for_each_cut(plan, tab, row, count, cut_block, act):
    if count == 1:
        act(0, 0)
        return
    which = tab[row, cut_block]
    index = tab[row + 1, cut_block]
    for ref in range(count):
        pl.when(which == ref)(functools.partial(act, ref, index))


def start_kernel_fetch(plan, tab, pieces, buf, sem, row_start, rows, col_start, cols):
    for tap in range(9):
        for block, at, to, length in segments(tap, row_start, rows, plan.C, plan.block_rows):

            def act(ref, index, tap=tap, at=at, to=to, length=length):
                pltpu.make_async_copy(
                    pieces[ref].at[index, pl.ds(at, length), pl.ds(col_start, cols)],
                    buf.at[tap, pl.ds(to, length)],
                    sem,
                ).start()

            for_each_cut(plan, tab, 0, plan.n_pieces, block, act)


def start_grad_store(plan, tab, buf, outs, sem, col_start, cols):
    for tap in range(9):
        for block, at, to, length in segments(tap, 0, plan.C, plan.C, plan.block_rows):

            def act(ref, index, tap=tap, at=at, to=to, length=length):
                pltpu.make_async_copy(
                    buf.at[tap, pl.ds(to, length)],
                    outs[ref].at[index, pl.ds(at, length), pl.ds(col_start, cols)],
                    sem,
                ).start()

            for_each_cut(plan, tab, 2, plan.n_outs, block, act)


def wait_for(buf, sem):
    pltpu.make_async_copy(buf, buf, sem).wait()


def edge_masks(plan):
    place = lax.broadcasted_iota(jnp.int32, (plan.R, LANES), 0) % plan.T
    return (place != 0).astype(F32), (place != plan.T - 1).astype(F32)


def interleave(dots, tasks):
    done = 0
    for i, dot in enumerate(dots):
        dot()
        upto = len(tasks) * (i + 1) // len(dots)
        for task in tasks[done:upto]:
            task()
        done = upto


def run_all(tasks):
    for task in tasks:
        task()


def store_split(high_ref, low_ref, at, value):
    high, low = split(value)
    high_ref[at] = high
    low_ref[at] = low


def patch_tasks(plan, xp, vh, vl, u):
    T = plan.T

    def task(lane, rb):
        rows, at = pl.ds(rb, 16), pl.ds(lane, LANES)
        line = []
        for col in range(3 * T + 2):
            if col in (0, 3 * T + 1):
                line.append(jnp.zeros((16, LANES), F32))
            else:
                line.append(patch_to_point(u, [xp.at[k, col - 1] for k in range(5)], (rows, at)))
        for j in range(T):
            for v, value in enumerate(patch_to_points(*line[3 * j : 3 * j + 5])):
                store_split(vh, vl, (u, v, j, rows, at), value)

    return [functools.partial(task, lane, rb) for lane in range(0, plan.C, LANES) for rb in range(0, plan.R, 16)]


def patch_to_point(u, planes, at):
    if u == 0:
        p1, p3 = planes[1][at], planes[3][at]
        return 2.0 * (planes[0][at] - planes[2][at]) + (p3 - p1)
    if u == 1:
        return (planes[3][at] - planes[2][at]) - 2.0 * planes[1][at]
    if u == 2:
        return 2.0 * planes[1][at] - 3.0 * planes[2][at] + planes[3][at]
    if u == 3:
        return planes[3][at] - planes[1][at]
    return (planes[4][at] - planes[2][at]) - 2.0 * (planes[3][at] - planes[1][at])


def cell_to_point(u, planes, at):
    if u == 0:
        return 0.5 * planes[0][at]
    if u == 1:
        return -0.5 * ((planes[0][at] + planes[2][at]) + planes[1][at])
    if u == 2:
        return (1.0 / 6.0) * (planes[1][at] - (planes[0][at] + planes[2][at]))
    if u == 3:
        return (1.0 / 6.0) * (planes[0][at] + 2.0 * (planes[1][at] + 2.0 * planes[2][at]))
    return planes[2][at]


def cell_tasks(plan, yb, wh, wl, u):
    def task(j, lane, rb):
        rows, at = pl.ds(rb, 16), pl.ds(lane, LANES)
        line = [cell_to_point(u, [yb.at[a, 3 * j + b] for a in range(3)], (rows, at)) for b in range(3)]
        for v, value in enumerate(cells_to_points(*line)):
            store_split(wh, wl, (v, j, rows, at), value)

    return [
        functools.partial(task, j, lane, rb)
        for j in range(plan.T)
        for lane in range(0, plan.N, LANES)
        for rb in range(0, plan.R, 16)
    ]


def tap_tasks(kbuf, uh, ul, point):
    def task(row):
        at = pl.ds(row, 16)
        parts = [taps_to_point(point, kbuf.at[q], kbuf.at[3 + q], kbuf.at[6 + q], at) for q in range(3)]
        for v, value in enumerate(taps_to_points(*parts)):
            store_split(uh, ul, (v, at), value)

    return [functools.partial(task, row) for row in range(0, kbuf.shape[1], 16)]


def dot_tasks(lefts, rights, dims, put):
    def dot(v):
        left = tuple(part.reshape(part.shape[0] * part.shape[1], part.shape[2]) for part in lefts(v))
        put(v, dot3(*left, *rights(v), dims))

    return [functools.partial(dot, v) for v in range(5)]


def forward_kernel(plan, last, tab, mask, bias, *refs):
    refs = list(refs)
    C, N, R, T = plan.C, plan.N, plan.R, plan.T
    cols = 3 * T
    x_hbm = refs.pop(0)
    cot_hbm = refs.pop(0) if last else None
    pieces = [refs.pop(0) for _ in range(plan.n_pieces)]
    act_hbm, slope_hbm, v_hbm = refs.pop(0), refs.pop(0), refs.pop(0)
    bias_sum = refs.pop(0) if last else None
    xp, vh, vl, kbuf, uh, ul, mbuf, ebuf, tail, x_sem, k_sem, out_sem, v_sem = refs[:13]
    cbuf, total, c_sem = refs[13:] if last else (None, None, None)
    chunks = C // N
    lanes = [pl.ds(lane, LANES) for lane in range(0, C, LANES)]

    def x_copy(i):
        return pltpu.make_async_copy(x_hbm.at[:, :, :, lanes[i]], xp.at[pl.ds(1, 3), :, :, lanes[i]], x_sem.at[i])

    def cot_copy(n):
        return pltpu.make_async_copy(cot_hbm.at[:, :, :, pl.ds(n * N, N)], cbuf, c_sem)

    def v_copies(u):
        return [
            pltpu.make_async_copy(part.at[u], v_hbm.at[which, u], v_sem.at[which, u])
            for which, part in enumerate((vh, vl))
        ]

    def out_copies(n):
        to = pl.ds(n * N, N)
        return [
            pltpu.make_async_copy(ebuf.at[n, pl.ds(0, 3)], act_hbm.at[:, :, :, to], out_sem.at[n, 0]),
            pltpu.make_async_copy(ebuf.at[n, pl.ds(3, 2)], slope_hbm.at[pl.ds(0, 2), :, :, to], out_sem.at[n, 1]),
            pltpu.make_async_copy(tail.at[n], slope_hbm.at[2, :, :, to], out_sem.at[n, 2]),
        ]

    for i in range(len(lanes)):
        x_copy(i).start()
    for n in range(chunks):
        start_kernel_fetch(plan, tab, pieces, kbuf.at[n], k_sem.at[n], 0, C, n * N, N)
    if last:
        cot_copy(0).start()
        total[...] = jnp.zeros((16, C), F32)
    not_first, not_last = edge_masks(plan)

    def shift(to, source, by, keep, at, col, _):
        xp[to, col, :, at] = pltpu.roll(xp[source, col, :, at], by, 0) * keep
        return 0

    first = patch_tasks(plan, xp, vh, vl, 0)
    per_lane = len(first) // len(lanes)
    for i, at in enumerate(lanes):
        x_copy(i).wait()
        lax.fori_loop(0, cols, functools.partial(shift, 0, 3, 1, not_first, at), 0)
        lax.fori_loop(0, cols, functools.partial(shift, 4, 1, R - 1, not_last, at), 0)
        run_all(first[i * per_lane : (i + 1) * per_lane])
    for copy in v_copies(0):
        copy.start()

    def column_task(n, u, j, rb):
        rows = pl.ds(rb, 16)
        cells = points_to_cells(*[mbuf[(n * 5 + u) % 2, v, j, rows] for v in range(5)])
        for b in range(3):
            ebuf[n, u, 3 * j + b, rows] = cells[b]

    def column_tasks(n, u):
        return [functools.partial(column_task, n, u, j, rb) for j in range(T) for rb in range(0, R, 16)]

    def finish_task(n, col, lane, rb):
        at, rows = pl.ds(lane, LANES), pl.ds(rb, 16)
        wide = pl.ds(n * N + lane, LANES)
        offset = bias[0:1, wide]
        cells = points_to_cells(*[ebuf[n, u, col, rows, at] for u in range(5)])
        sums = None
        for a in range(3):
            value, slope = gelu_parts(cells[a] + offset)
            keep = mask[a, col, rows]
            slope = slope * keep
            if last:
                slope = slope * cbuf[a, col, rows, at]
                sums = slope if sums is None else sums + slope
            ebuf[n, a, col, rows, at] = value * keep
            if a < 2:
                ebuf[n, 3 + a, col, rows, at] = slope
            else:
                tail[n, col, rows, at] = slope
        if last:
            total[:, wide] += sums

    def finish_tasks(n):
        return [
            functools.partial(finish_task, n, col, lane, rb)
            for col in range(cols)
            for lane in range(0, N, LANES)
            for rb in range(0, R, 16)
        ]

    steps = [(n, u) for n in range(chunks) for u in range(5)]
    wait_for(kbuf.at[0], k_sem.at[0])
    run_all(tap_tasks(kbuf.at[0], uh.at[0], ul.at[0], 0))
    for s, (n, u) in enumerate(steps):
        tasks = []
        if n > 0 and u == 0:
            finishing = finish_tasks(n - 1)
            if last:
                cot_copy(n - 1).wait()
        if s + 1 < len(steps):
            next_n, next_u = steps[s + 1]
            if next_u == 0:
                wait_for(kbuf.at[next_n], k_sem.at[next_n])
            if n == 0 and u < 4:
                tasks += patch_tasks(plan, xp, vh, vl, u + 1)
            tasks += tap_tasks(kbuf.at[next_n], uh.at[(s + 1) % 2], ul.at[(s + 1) % 2], next_u)
        if s > 0:
            tasks = column_tasks(*steps[s - 1]) + tasks
        if n > 0 and u > 0:
            count = len(finishing)
            tasks += finishing[count * (u - 1) // 4 : count * u // 4]

        def put(v, value, s=s):
            mbuf[s % 2, v] = value.reshape(T, R, N)

        interleave(
            dot_tasks(
                lambda v: (vh[u, v], vl[u, v]),
                lambda v: (uh[s % 2, v], ul[s % 2, v]),
                NN,
                put,
            ),
            tasks,
        )
        if n == 0 and u < 4:
            for copy in v_copies(u + 1):
                copy.start()
        if n > 0 and u == 4:
            for copy in out_copies(n - 1):
                copy.start()
            if last:
                cot_copy(n).start()
    run_all(column_tasks(*steps[-1]))
    n = chunks - 1
    if last:
        cot_copy(n).wait()
    run_all(finish_tasks(n))
    for copy in out_copies(n):
        copy.start()
    if last:
        bias_sum[...] = jnp.sum(total[...], axis=0, keepdims=True)
    for u in range(5):
        for copy in v_copies(u):
            copy.wait()
    for n in range(chunks):
        for copy in out_copies(n):
            copy.wait()


def back_kernel(plan, last, tab, mask, *refs):
    refs = list(refs)
    C, N, R, T = plan.C, plan.N, plan.R, plan.T
    cols = 3 * T
    chunks = C // N
    w_hbm = refs.pop(0)
    slope_hbm = None if last else refs.pop(0)
    pieces = [refs.pop(0) for _ in range(plan.n_pieces)]
    out_hbm = refs.pop(0)
    bias_sum = None if last else refs.pop(0)
    wh, wl, kbuf, uh, ul, mbuf, ebuf, w_sem, k_sem, out_sem = refs[:10]
    sbuf, total, s_sem = (None, None, None) if last else refs[10:]

    def w_copies(u):
        return [
            pltpu.make_async_copy(w_hbm.at[which, u], part.at[u], w_sem.at[which, u])
            for which, part in enumerate((wh, wl))
        ]

    def slope_copy(n):
        return pltpu.make_async_copy(slope_hbm.at[:, :, :, pl.ds(n * N, N)], sbuf, s_sem)

    def out_copy(n):
        return pltpu.make_async_copy(ebuf.at[n, pl.ds(0, 3)], out_hbm.at[:, :, :, pl.ds(n * N, N)], out_sem.at[n])

    start_kernel_fetch(plan, tab, pieces, kbuf.at[0], k_sem.at[0], 0, N, 0, C)
    for u in range(5):
        for copy in w_copies(u):
            copy.start()
    for n in range(1, chunks):
        start_kernel_fetch(plan, tab, pieces, kbuf.at[n], k_sem.at[n], n * N, N, 0, C)
    if not last:
        slope_copy(0).start()
        total[...] = jnp.zeros((R, C), F32)
    not_first, not_last = edge_masks(plan)
    for parity in range(2):
        for v in (0, 4):
            mbuf[parity, v, 0] = jnp.zeros((R, N), F32)
            mbuf[parity, v, T + 1] = jnp.zeros((R, N), F32)

    def column_task(n, u, j, rb):
        rows = pl.ds(rb, 16)
        parity = (n * 5 + u) % 2
        here = points_to_patch(*[mbuf[parity, v, j + 1, rows] for v in range(5)])
        ebuf[n, u, 3 * j, rows] = here[0] + mbuf[parity, 4, j, rows]
        ebuf[n, u, 3 * j + 1, rows] = here[1]
        ebuf[n, u, 3 * j + 2, rows] = here[2] + 2.0 * mbuf[parity, 0, j + 2, rows]

    def column_tasks(n, u):
        return [functools.partial(column_task, n, u, j, rb) for j in range(T) for rb in range(0, R, 16)]

    def finish_task(n, col, lane):
        at = pl.ds(lane, LANES)
        wide = pl.ds(n * N + lane, LANES)
        points = [ebuf[n, u, col, :, at] for u in range(5)]
        here = points_to_patch(*points)
        cells = (
            here[0] + pltpu.roll(points[4], 1, 0) * not_first,
            here[1],
            here[2] + 2.0 * (pltpu.roll(points[0], R - 1, 0) * not_last),
        )
        sums = None
        for a in range(3):
            back = cells[a] * (mask[a, col] if last else sbuf[a, col, :, at])
            ebuf[n, a, col, :, at] = back
            sums = back if sums is None else sums + back
        if not last:
            total[:, wide] += sums

    def finish_tasks(n):
        return [functools.partial(finish_task, n, col, lane) for col in range(cols) for lane in range(0, N, LANES)]

    steps = [(n, u) for n in range(chunks) for u in range(5)]
    wait_for(kbuf.at[0], k_sem.at[0])
    run_all(tap_tasks(kbuf.at[0], uh.at[0], ul.at[0], 0))
    for s, (n, u) in enumerate(steps):
        tasks = []
        if n == 0:
            for copy in w_copies(u):
                copy.wait()
        if n > 0 and u == 0:
            finishing = finish_tasks(n - 1)
            if not last:
                slope_copy(n - 1).wait()
        if s + 1 < len(steps):
            next_n, next_u = steps[s + 1]
            if next_u == 0:
                wait_for(kbuf.at[next_n], k_sem.at[next_n])
            tasks += tap_tasks(kbuf.at[next_n], uh.at[(s + 1) % 2], ul.at[(s + 1) % 2], next_u)
        if s > 0:
            tasks = column_tasks(*steps[s - 1]) + tasks
        if n > 0 and u > 0:
            count = len(finishing)
            tasks += finishing[count * (u - 1) // 4 : count * u // 4]

        def put(v, value, s=s):
            mbuf[s % 2, v, pl.ds(1, T)] = value.reshape(T, R, N)

        interleave(
            dot_tasks(
                lambda v: (wh[u, v], wl[u, v]),
                lambda v: (uh[s % 2, v], ul[s % 2, v]),
                NT,
                put,
            ),
            tasks,
        )
        if n > 0 and u == 4:
            out_copy(n - 1).start()
            if not last:
                slope_copy(n).start()
    run_all(column_tasks(*steps[-1]))
    n = chunks - 1
    if not last:
        slope_copy(n).wait()
    run_all(finish_tasks(n))
    out_copy(n).start()
    if not last:
        bias_sum[...] = jnp.sum(total[...], axis=0, keepdims=True)
    for n in range(chunks):
        out_copy(n).wait()


def grad_kernel(plan, tab, bias_rows, v_hbm, y_hbm, *refs):
    refs = list(refs)
    C, N, R, T = plan.C, plan.N, plan.R, plan.T
    chunks = C // N
    outs = [refs.pop(0) for _ in range(plan.n_outs)]
    w_hbm = refs.pop(0)
    vh, vl, yb, wh, wl, dbuf, kgrad, v_sem, y_sem, w_sem, out_sem, bias_sem = refs

    def v_copies(u):
        return [
            pltpu.make_async_copy(v_hbm.at[which, u], part.at[u], v_sem.at[which, u])
            for which, part in enumerate((vh, vl))
        ]

    def y_copy(n):
        return pltpu.make_async_copy(y_hbm.at[:, :, :, pl.ds(n * N, N)], yb.at[n], y_sem.at[n])

    def w_copies(s):
        n, u = steps[s]
        return [
            pltpu.make_async_copy(
                part.at[s % 3], w_hbm.at[which, u, :, :, :, pl.ds(n * N, N)], w_sem.at[which, s % 3]
            )
            for which, part in enumerate((wh, wl))
        ]

    def add_task(n, u, row):
        at = pl.ds(row, 16)
        taps = points_to_taps(*[dbuf[(n * 5 + u) % 2, v, at] for v in range(5)])
        for p, weight in POINT_TAPS[u]:
            for q in range(3):
                term = taps[q] if weight == 1.0 else weight * taps[q]
                if u == 0 or (u == 1 and p > 0):
                    kgrad[n, 3 * p + q, at] = term
                else:
                    kgrad[n, 3 * p + q, at] += term

    def add_tasks(n, u):
        return [functools.partial(add_task, n, u, row) for row in range(0, C, 16)]

    def bias_copies():
        if plan.n_outs == 1:
            return []
        blocks = 9 * C // plan.block_rows // plan.n_outs
        return [
            pltpu.make_async_copy(bias_rows, out.at[i, pl.ds(plan.block_rows, 8)], bias_sem)
            for out in outs
            for i in range(blocks)
        ]

    steps = [(n, u) for n in range(chunks) for u in range(5)]
    y_copy(0).start()
    for u in range(5):
        for copy in v_copies(u):
            copy.start()
    for n in range(1, chunks):
        y_copy(n).start()
    for copy in bias_copies():
        copy.start()
    y_copy(0).wait()
    run_all(cell_tasks(plan, yb.at[0], wh.at[0], wl.at[0], 0))
    for s, (n, u) in enumerate(steps):
        for copy in w_copies(s):
            copy.start()
        tasks = []
        if n == 0:
            for copy in v_copies(u):
                copy.wait()
        if s > 0:
            tasks += add_tasks(*steps[s - 1])
        if s + 1 < len(steps):
            if s >= 2:
                for copy in w_copies(s - 2):
                    copy.wait()
            next_n, next_u = steps[s + 1]
            if next_u == 0:
                y_copy(next_n).wait()
            tasks += cell_tasks(plan, yb.at[next_n], wh.at[(s + 1) % 3], wl.at[(s + 1) % 3], next_u)

        def put(v, value, s=s):
            dbuf[s % 2, v] = value

        def rights(v, s=s):
            return tuple(part[s % 3, v].reshape(T * R, N) for part in (wh, wl))

        interleave(dot_tasks(lambda v: (vh[u, v], vl[u, v]), rights, TN, put), tasks)
        if n > 0 and u == 0:
            start_grad_store(plan, tab, kgrad.at[n - 1], outs, out_sem.at[n - 1], (n - 1) * N, N)
    run_all(add_tasks(*steps[-1]))
    n = chunks - 1
    start_grad_store(plan, tab, kgrad.at[n], outs, out_sem.at[n], n * N, N)
    for s in range(max(0, len(steps) - 3), len(steps)):
        for copy in w_copies(s):
            copy.wait()
    for copy in bias_copies():
        copy.wait()
    for n in range(chunks):
        wait_for(kgrad.at[n], out_sem.at[n])


SMEM_SPEC = pl.BlockSpec(memory_space=pltpu.SMEM)
VMEM_SPEC = pl.BlockSpec(memory_space=pltpu.VMEM)
ANY_SPEC = pl.BlockSpec(memory_space=pl.ANY)


def plane_shape(plan):
    return jax.ShapeDtypeStruct((3, 3 * plan.T, plan.R, plan.C), F32)


def point_scratch(plan, width):
    shape = (5, 5, plan.T, plan.R, width)
    return [pltpu.VMEM(shape, BF16), pltpu.VMEM(shape, BF16)]


def call(kernel, outs, in_specs, out_specs, scratch, flops, args, name):
    moved = sum(a.size * a.dtype.itemsize for a in args) + sum(o.size * 4 for o in outs)
    return pl.pallas_call(
        kernel,
        out_shape=outs,
        in_specs=in_specs,
        out_specs=out_specs,
        scratch_shapes=scratch,
        compiler_params=pltpu.CompilerParams(vmem_limit_bytes=VMEM_LIMIT),
        cost_estimate=pl.CostEstimate(flops=flops, bytes_accessed=moved, transcendentals=0),
        name=name,
    )(*args)


def pass_flops(plan):
    return 2 * 3 * 25 * plan.T * plan.R * plan.C * plan.C


def point_shape(plan):
    return jax.ShapeDtypeStruct((2, 5, 5, plan.T, plan.R, plan.C), BF16)


def run_forward(plan, tab, mask, bias, x, cot, pieces, name):
    last = cot is not None
    C, N, R, T = plan.C, plan.N, plan.R, plan.T
    cols = 3 * T
    chunks = C // N
    outs = [plane_shape(plan), plane_shape(plan), point_shape(plan)]
    out_specs = [ANY_SPEC, ANY_SPEC, ANY_SPEC]
    scratch = [
        pltpu.VMEM((5, cols, R, C), F32),
        *point_scratch(plan, C),
        pltpu.VMEM((chunks, 9, C, N), F32),
        pltpu.VMEM((2, 5, C, N), BF16),
        pltpu.VMEM((2, 5, C, N), BF16),
        pltpu.VMEM((2, 5, T, R, N), F32),
        pltpu.VMEM((chunks, 5, cols, R, N), F32),
        pltpu.VMEM((chunks, cols, R, N), F32),
        pltpu.SemaphoreType.DMA((C // LANES,)),
        pltpu.SemaphoreType.DMA((chunks,)),
        pltpu.SemaphoreType.DMA((chunks, 3)),
        pltpu.SemaphoreType.DMA((2, 5)),
    ]
    args = [tab, mask, bias, x]
    if last:
        outs.append(jax.ShapeDtypeStruct((1, C), F32))
        out_specs.append(VMEM_SPEC)
        scratch += [pltpu.VMEM((3, cols, R, N), F32), pltpu.VMEM((16, C), F32), pltpu.SemaphoreType.DMA]
        args.append(cot)
    args += pieces
    in_specs = [SMEM_SPEC, VMEM_SPEC, VMEM_SPEC] + [ANY_SPEC] * (len(args) - 3)
    kernel = functools.partial(forward_kernel, plan, last)
    return call(kernel, outs, in_specs, out_specs, scratch, pass_flops(plan), args, name)


def run_back(plan, tab, mask, points, slope, pieces, name):
    last = slope is None
    C, N, R, T = plan.C, plan.N, plan.R, plan.T
    cols = 3 * T
    chunks = C // N
    outs = [plane_shape(plan)]
    out_specs = [ANY_SPEC]
    scratch = [
        *point_scratch(plan, C),
        pltpu.VMEM((chunks, 9, N, C), F32),
        pltpu.VMEM((2, 5, N, C), BF16),
        pltpu.VMEM((2, 5, N, C), BF16),
        pltpu.VMEM((2, 5, T + 2, R, N), F32),
        pltpu.VMEM((chunks, 5, cols, R, N), F32),
        pltpu.SemaphoreType.DMA((2, 5)),
        pltpu.SemaphoreType.DMA((chunks,)),
        pltpu.SemaphoreType.DMA((chunks,)),
    ]
    args = [tab, mask, points]
    if not last:
        outs.append(jax.ShapeDtypeStruct((1, C), F32))
        out_specs.append(VMEM_SPEC)
        scratch += [pltpu.VMEM((3, cols, R, N), F32), pltpu.VMEM((R, C), F32), pltpu.SemaphoreType.DMA]
        args.append(slope)
    args += pieces
    in_specs = [SMEM_SPEC, VMEM_SPEC] + [ANY_SPEC] * (len(args) - 2)
    kernel = functools.partial(back_kernel, plan, last)
    return call(kernel, outs, in_specs, out_specs, scratch, pass_flops(plan), args, name)


def run_grad(plan, tab, bias_rows, points, y, name):
    C, N, R, T = plan.C, plan.N, plan.R, plan.T
    cols = 3 * T
    chunks = C // N
    blocks = 9 * C // plan.block_rows // plan.n_outs
    block = plan.block_rows + (8 if plan.n_outs == 2 else 0)
    outs = [jax.ShapeDtypeStruct((blocks, block, C), F32) for _ in range(plan.n_outs)]
    outs.append(point_shape(plan))
    scratch = [
        *point_scratch(plan, C),
        pltpu.VMEM((chunks, 3, cols, R, N), F32),
        pltpu.VMEM((3, 5, T, R, N), BF16),
        pltpu.VMEM((3, 5, T, R, N), BF16),
        pltpu.VMEM((2, 5, C, N), F32),
        pltpu.VMEM((chunks, 9, C, N), F32),
        pltpu.SemaphoreType.DMA((2, 5)),
        pltpu.SemaphoreType.DMA((chunks,)),
        pltpu.SemaphoreType.DMA((2, 3)),
        pltpu.SemaphoreType.DMA((chunks,)),
        pltpu.SemaphoreType.DMA,
    ]
    in_specs = [SMEM_SPEC, VMEM_SPEC, ANY_SPEC, ANY_SPEC]
    kernel = functools.partial(grad_kernel, plan)
    return call(kernel, outs, in_specs, [ANY_SPEC] * len(outs), scratch, pass_flops(plan), [tab, bias_rows, points, y], name)


def to_planes(plan, cells):
    slots, side, _, channels = cells.shape
    tiled = cells.reshape(slots, plan.T, 3, side, channels).transpose(2, 3, 0, 1, 4)
    flat = tiled.reshape(3, side, slots * plan.T, channels)
    return jnp.pad(flat, ((0, 0), (0, 0), (0, plan.R - slots * plan.T), (0, 0)))


def from_planes(plan, planes, slots):
    side = 3 * plan.T
    kept = planes[:, :, : slots * plan.T].reshape(3, side, slots, plan.T, planes.shape[3])
    return kept.transpose(2, 3, 0, 1, 4).reshape(slots, side, side, planes.shape[3])


def tie(*values):
    return lax.optimization_barrier(values)


class Net:
    def __init__(self):
        self.rep = lax.axis_size("rep")
        self.dp = lax.axis_size("dp")
        self.routed = self.rep == 4 and self.dp == 8
        self.n_pieces = 4 if self.routed else 1
        self.n_outs = 2 if self.routed else 1

    def perm(self, move):
        pairs = []
        for x in range(2):
            for c in range(2):
                for z in range(4):
                    for y in range(2):
                        to = move(x, c, z, y)
                        pairs.append((((x * 2 + c) * 4 + z) * 2 + y, ((to[0] * 2 + to[1]) * 4 + to[2]) * 2 + to[3]))
        return pairs

    def send(self, value, move):
        return lax.ppermute(value, AXES, self.perm(move))

    def over_core(self, value):
        return self.send(value, lambda x, c, z, y: (x, 1 - c, z, y))

    def over_first(self, value):
        return self.send(value, lambda x, c, z, y: (x, c, z, 1 - y) if c == 0 else (1 - x, c, z, y))

    def over_second(self, value):
        return self.send(value, lambda x, c, z, y: (1 - x, c, z, y) if c == 0 else (x, c, z, 1 - y))

    def over_z(self, value, step):
        return self.send(value, lambda x, c, z, y: (x, c, (z + step) % 4, y))

    def tables(self):
        if not self.routed:
            return jnp.zeros((4, 8), jnp.int32)
        rep = lax.axis_index("rep")
        dp = lax.axis_index("dp")
        x, c, z, y = rep // 2, rep % 2, dp // 2, dp % 2
        block = jnp.arange(32, dtype=jnp.int32)
        bx, bc, bz, by = block // 16, block // 8 % 2, block // 2 % 4, block % 2
        dx, dy = bx ^ x, by ^ y
        second = jnp.where(bc == 0, dx, dy)
        first = jnp.where(bc == 0, dy, dx)
        other = (bc != c).astype(jnp.int32)
        return jnp.stack(
            [2 * other + second, 4 * first + (z - bz) % 4, other, 8 * second + 4 * first + (bz - z) % 4]
        ).astype(jnp.int32)

    def gather_z(self, shard):
        return jnp.stack([shard] + [self.over_z(shard, step) for step in (1, 2, 3)])

    def gather_whole(self, shard):
        return [lax.all_gather(shard, AXES, axis=0, tiled=True)[None]]

    def sum_whole(self, parts):
        return lax.psum_scatter(parts[0][0], AXES, scatter_dimension=0, tiled=True)

    def send_z(self, four):
        return [four[0]] + [self.over_z(four[step], step) for step in (1, 2, 3)]


def body(
    features, map_size, item_count, conv4_weight, conv4_bias, conv5_weight, conv5_bias, cotangent
):
    slots, side, _, channels = features.shape
    net = Net()
    tiles = side // 3
    rows = -(-slots * tiles // 16) * 16
    shard_rows = conv4_weight.shape[0] // channels
    block_rows = shard_rows if net.routed else 9 * channels
    plan = Plan(channels, rows, tiles, block_rows, net.n_pieces, net.n_outs)

    live = jnp.arange(slots, dtype=jnp.int32) < item_count[0]
    inside = jnp.arange(side, dtype=jnp.int32)[None, :] < map_size[:, None]
    valid = live[:, None, None] & inside[:, :, None] & inside[:, None, :]
    mask = to_planes(plan, jnp.broadcast_to(valid.astype(F32)[..., None], (slots, side, side, LANES)))
    source = to_planes(plan, features * valid.astype(F32)[..., None])
    cot = to_planes(plan, cotangent)
    tab = net.tables()

    shard4 = conv4_weight.reshape(shard_rows, channels)
    shard5 = conv5_weight.reshape(shard_rows, channels)
    if net.routed:
        four4 = net.gather_z(shard4)
        shard5, four4 = tie(shard5, four4)
        four5 = net.gather_z(shard5)
        eight4 = jnp.concatenate([four4, net.over_first(four4)])
        far4 = net.over_second(eight4)
        four5, far4, eight4 = tie(four5, far4, eight4)
        pieces4 = [eight4, far4, net.over_core(eight4), net.over_core(far4)]
        eight5 = jnp.concatenate([four5, net.over_first(four5)])
        eight5, source = tie(eight5, source)
        far5 = net.over_second(eight5)
        near5 = net.over_core(eight5)
    else:
        pieces4 = net.gather_whole(shard4)
        pieces5 = net.gather_whole(shard5)
    hidden, slope4, points4 = run_forward(plan, tab, mask, conv4_bias[None], source, None, pieces4, "conv4")
    if net.routed:
        far5, near5, hidden = tie(far5, near5, hidden)
        pieces5 = [eight5, far5, near5, net.over_core(far5)]
    out5, back5, points5, bias5 = run_forward(plan, tab, mask, conv5_bias[None], hidden, cot, pieces5, "conv5")
    *grad5, cells5 = run_grad(plan, tab, jnp.pad(bias5, ((0, 7), (0, 0))), points5, back5, "grad5")
    if net.routed:
        got = net.over_core(grad5[1])
        keep5, send5 = grad5[0][:8] + got[:8], grad5[0][8:] + got[8:]
        keep5, send5, cells5 = tie(keep5, send5, cells5)
        got5 = net.over_second(send5)
    back4, bias4 = run_back(plan, tab, mask, cells5, slope4, pieces5, "back5")
    if net.routed:
        got5, back4 = tie(got5, back4)
        keep5, send5 = keep5[:4] + got5[:4], keep5[4:] + got5[4:]
        keep5, send5, back4 = tie(keep5, send5, back4)
        got5 = net.over_first(send5)
    *grad4, cells4 = run_grad(plan, tab, jnp.pad(bias4, ((0, 7), (0, 0))), points4, back4, "grad4")
    if net.routed:
        got5, *grad4 = tie(got5, *grad4)
        got = net.over_core(grad4[1])
        keep4, send4 = grad4[0][:8] + got[:8], grad4[0][8:] + got[8:]
        four5 = keep5 + got5
        keep4, send4, four5, cells4 = tie(keep4, send4, four5, cells4)
        got5 = net.send_z(four5)
        got4 = net.over_second(send4)
    input_grad = run_back(plan, tab, mask, cells4, None, pieces4, "back4")[0]
    if net.routed:
        got4, input_grad, *got5 = tie(got4, input_grad, *got5)
        keep4, send4 = keep4[:4] + got4[:4], keep4[4:] + got4[4:]
        sum4 = sum(net.send_z(keep4 + net.over_first(send4)))
        sum5 = sum(got5)
        share4, total4 = sum4[:shard_rows], sum4[shard_rows]
        share5, total5 = sum5[:shard_rows], sum5[shard_rows]
    else:
        share5 = net.sum_whole(grad5)
        share4 = net.sum_whole(grad4)
        total4, total5 = lax.psum((bias4[0], bias5[0]), AXES)

    total_cells = slots * net.rep * net.dp * side * side
    scale = float(total_cells) ** (-0.5)
    return (
        from_planes(plan, out5, slots),
        from_planes(plan, input_grad, slots),
        (share4 * scale).reshape(-1),
        total4 * scale,
        (share5 * scale).reshape(-1),
        total5 * scale,
    )


def solution(mesh):
    placed = (
        P(AXES, None, None, None),
        P(AXES),
        P(AXES),
        P(AXES),
        P(),
        P(AXES),
        P(),
        P(AXES, None, None, None),
    )
    return jax.shard_map(
        body,
        mesh=mesh,
        in_specs=placed,
        out_specs=(
            P(AXES, None, None, None),
            P(AXES, None, None, None),
            P(AXES),
            P(),
            P(AXES),
            P(),
        ),
        check_vma=False,
    )
```

```python
import functools

import jax
import jax.numpy as jnp
from jax import lax
from jax.experimental import pallas as pl
from jax.experimental.pallas import tpu as pltpu
from jax.sharding import PartitionSpec as P

AXES = ("rep", "dp")
F32 = jnp.float32
BF16 = jnp.bfloat16
LANES = 128
VMEM_LIMIT = 62 * 2**20
NN = (((1,), (0,)), ((), ()))
NT = (((1,), (1,)), ((), ()))
TN = (((0,), (0,)), ((), ()))
GELU_K = 0.7978845608028654
GELU_C = 0.044715


def patch_to_points(p0, p1, p2, p3, p4):
    d = p3 - p1
    return (
        (p0 - p2) + 0.5 * d,
        p1 + 0.5 * (p2 - p3),
        0.5 * p2 - (1.0 / 6.0) * (p1 + p1 + p3),
        (1.0 / 6.0) * d,
        (p4 - p2) - 2.0 * d,
    )


def points_to_patch(n0, n1, n2, n3, n4):
    e = 0.5 * n0 - 2.0 * n4
    f = (1.0 / 6.0) * n3
    g = (1.0 / 6.0) * n2
    return (
        (n1 - e) - (g + g + f),
        0.5 * (n1 + n2) - (n0 + n4),
        (e - 0.5 * n1) + (f - g),
    )


def taps_to_points(k0, k1, k2):
    s = k0 + k2
    return (k0, s + k1, s - k1, k0 + 2.0 * (k1 + 2.0 * k2), k2)


def taps_to_point(index, k0, k1, k2, at):
    if index == 0:
        return k0[at]
    if index == 1:
        return (k0[at] + k2[at]) + k1[at]
    if index == 2:
        return (k0[at] + k2[at]) - k1[at]
    if index == 3:
        return k0[at] + 2.0 * (k1[at] + 2.0 * k2[at])
    return k2[at]


POINT_TAPS = (((0, 1.0),), ((0, 1.0), (1, 1.0), (2, 1.0)), ((0, 1.0), (1, -1.0), (2, 1.0)), ((0, 1.0), (1, 2.0), (2, 4.0)), ((2, 1.0),))


def points_to_taps(d0, d1, d2, d3, d4):
    s = d1 + d2
    return (d0 + s + d3, (d1 - d2) + 2.0 * d3, s + 4.0 * d3 + d4)


def split(value):
    high = value.astype(BF16)
    return high, (value - high.astype(F32)).astype(BF16)


def dot3(left_high, left_low, right_high, right_low, dims):
    def dot(left, right):
        return lax.dot_general(left, right, dims, preferred_element_type=F32)

    return dot(left_high, right_high) + dot(left_low, right_high) + dot(left_high, right_low)


def gelu_parts(v):
    square = v * v
    half = 0.5 + 0.5 * jnp.tanh(v * (GELU_K + (GELU_K * GELU_C) * square))
    value = v * half
    return value, half + value * ((1.0 - half) * (2.0 * GELU_K + (6.0 * GELU_K * GELU_C) * square))


def segments(tap, start, rows, tap_rows, block_rows):
    cuts = []
    at = tap * tap_rows + start
    end = at + rows
    first = at
    while at < end:
        block = at // block_rows
        stop = min(end, (block + 1) * block_rows)
        cuts.append((block, at - block * block_rows, at - first, stop - at))
        at = stop
    return cuts


class Plan:
    def __init__(self, channels, rows, tiles, block_rows, n_pieces, n_outs):
        self.C = channels
        self.R = rows
        self.T = tiles
        self.block_rows = block_rows
        self.n_pieces = n_pieces
        self.n_outs = n_outs
        self.N = min(256, channels)


def for_each_cut(plan, tab, row, count, cut_block, act):
    if count == 1:
        act(0, 0)
        return
    which = tab[row, cut_block]
    index = tab[row + 1, cut_block]
    for ref in range(count):
        pl.when(which == ref)(functools.partial(act, ref, index))


def start_kernel_fetch(plan, tab, pieces, buf, sem, row_start, rows, col_start, cols):
    for first in range(0, len(pieces), plan.n_pieces):
        group = pieces[first : first + plan.n_pieces]
        width = group[0].shape[2]
        group_start = first // plan.n_pieces * width
        low = max(col_start, group_start)
        high = min(col_start + cols, group_start + width)
        if low >= high:
            continue
        for tap in range(9):
            for block, at, to, length in segments(tap, row_start, rows, plan.C, plan.block_rows):

                def act(ref, index, tap=tap, at=at, to=to, length=length):
                    pltpu.make_async_copy(
                        group[ref].at[index, pl.ds(at, length), pl.ds(low - group_start, high - low)],
                        buf.at[tap, pl.ds(to, length), pl.ds(low - col_start, high - low)],
                        sem,
                    ).start()

                for_each_cut(plan, tab, 0, plan.n_pieces, block, act)


def start_grad_store(plan, tab, buf, folded, outs, sem, col_start):
    N = plan.N
    for tap in range(9):
        for start in range(0, plan.C, N):
            for block, at, to, length in segments(tap, start, N, plan.C, plan.block_rows):
                if folded:
                    part = buf.at[tap, pl.ds(to, length), pl.ds(start, N)]
                else:
                    part = buf.at[tap, pl.ds(start + to, length)]

                def act(ref, index, part=part, at=at, length=length):
                    pltpu.make_async_copy(
                        part, outs[ref].at[index, pl.ds(at, length), pl.ds(col_start, N)], sem
                    ).start()

                for_each_cut(plan, tab, 2, plan.n_outs, block, act)


def wait_for(buf, sem):
    pltpu.make_async_copy(buf, buf, sem).wait()


def edge_masks(plan):
    place = lax.broadcasted_iota(jnp.int32, (plan.R, LANES), 0) % plan.T
    return (place != 0).astype(F32), (place != plan.T - 1).astype(F32)


def interleave(dots, tasks):
    done = 0
    for i, dot in enumerate(dots):
        dot()
        upto = len(tasks) * (i + 1) // len(dots)
        for task in tasks[done:upto]:
            task()
        done = upto


def run_all(tasks):
    for task in tasks:
        task()


def store_split(high_ref, low_ref, at, value):
    high, low = split(value)
    high_ref[at] = high
    low_ref[at] = low


def patch_tasks(plan, xp, vh, vl, u):
    T = plan.T

    def task(lane, rb):
        rows, at = pl.ds(rb, 16), pl.ds(lane, LANES)
        line = []
        for col in range(3 * T + 2):
            if col in (0, 3 * T + 1):
                line.append(jnp.zeros((16, LANES), F32))
            else:
                line.append(patch_to_point(u, [xp.at[k, col - 1] for k in range(5)], (rows, at)))
        for j in range(T):
            for v, value in enumerate(patch_to_points(*line[3 * j : 3 * j + 5])):
                store_split(vh, vl, (u, v, j, rows, at), value)

    return [functools.partial(task, lane, rb) for lane in range(0, plan.C, LANES) for rb in range(0, plan.R, 16)]


def patch_to_point(u, planes, at):
    if u == 0:
        return (planes[0][at] - planes[2][at]) + 0.5 * (planes[3][at] - planes[1][at])
    if u == 1:
        return planes[1][at] + 0.5 * (planes[2][at] - planes[3][at])
    if u == 2:
        p1 = planes[1][at]
        return 0.5 * planes[2][at] - (1.0 / 6.0) * (p1 + p1 + planes[3][at])
    if u == 3:
        return (1.0 / 6.0) * (planes[3][at] - planes[1][at])
    return (planes[4][at] - planes[2][at]) - 2.0 * (planes[3][at] - planes[1][at])


def cell_tasks(plan, planes, wh, wl, u):
    def task(lane, j, rb):
        rows, at = pl.ds(rb, 16), pl.ds(lane, LANES)
        line = [taps_to_point(u, *[plane.at[3 * j + b] for plane in planes], (rows, at)) for b in range(3)]
        for v, value in enumerate(taps_to_points(*line)):
            store_split(wh, wl, (v, j, rows, at), value)

    return [
        functools.partial(task, lane, j, rb)
        for lane in range(0, planes[0].shape[2], LANES)
        for j in range(plan.T)
        for rb in range(0, plan.R, 16)
    ]


def tap_tasks(kbuf, uh, ul, point):
    def task(row):
        at = pl.ds(row, 16)
        parts = [taps_to_point(point, kbuf.at[q], kbuf.at[3 + q], kbuf.at[6 + q], at) for q in range(3)]
        for v, value in enumerate(taps_to_points(*parts)):
            store_split(uh, ul, (v, at), value)

    return [functools.partial(task, row) for row in range(0, kbuf.shape[1], 16)]


def dot_tasks(lefts, rights, dims, put):
    def dot(v):
        left = tuple(part.reshape(part.shape[0] * part.shape[1], part.shape[2]) for part in lefts(v))
        put(v, dot3(*left, *rights(v), dims))

    return [functools.partial(dot, v) for v in range(5)]


class GradSteps:
    def __init__(self, plan, tab, vh, vl, planes_of, wh, wl, dbuf, grads, folded, outs, out_sem):
        self.plan, self.tab, self.vh, self.vl, self.planes_of = plan, tab, vh, vl, planes_of
        self.wh, self.wl, self.dbuf, self.grads, self.folded = wh, wl, dbuf, grads, folded
        self.outs, self.out_sem = outs, out_sem
        self.steps = [(n, u) for n in range(plan.C // plan.N) for u in range(5)]

    def cells(self, s):
        n, u = self.steps[s]
        return cell_tasks(self.plan, self.planes_of(n), self.wh.at[s % 2], self.wl.at[s % 2], u)

    def add(self, s, row):
        n, u = self.steps[s]
        plan, grad = self.plan, self.grads.at[n]
        taps = points_to_taps(*[self.dbuf[s % 2, v, pl.ds(row, 16)] for v in range(5)])
        if self.folded:
            place = (pl.ds(row % plan.N, 16), pl.ds(row // plan.N * plan.N, plan.N))
        else:
            place = (pl.ds(row, 16), slice(None))
        for k, weight in POINT_TAPS[u]:
            for q in range(3):
                term = taps[q] if weight == 1.0 else weight * taps[q]
                if u == 0 or (u == 1 and k > 0):
                    grad[(3 * k + q, *place)] = term
                else:
                    grad[(3 * k + q, *place)] += term

    def adds(self, s):
        return [functools.partial(self.add, s, row) for row in range(0, self.plan.C, 16)]

    def dots(self, s):
        n, u = self.steps[s]
        rows = self.plan.T * self.plan.R

        def put(v, value):
            self.dbuf[s % 2, v] = value

        def rights(v):
            return tuple(part[s % 2, v].reshape(rows, self.plan.N) for part in (self.wh, self.wl))

        return dot_tasks(lambda v: (self.vh[u, v], self.vl[u, v]), rights, TN, put)

    def store(self, n):
        start_grad_store(
            self.plan, self.tab, self.grads.at[n], self.folded, self.outs, self.out_sem.at[n], n * self.plan.N
        )

    def wait(self):
        for n in range(self.plan.C // self.plan.N):
            wait_for(self.grads.at[n], self.out_sem.at[n])


def bias_copies(plan, rows, outs, sem):
    if plan.n_outs == 1:
        return []
    return [
        pltpu.make_async_copy(rows, out.at[i, pl.ds(plan.block_rows, 8)], sem)
        for out in outs
        for i in range(out.shape[0])
    ]


def part_of(tasks, index, count):
    return tasks[len(tasks) * index // count : len(tasks) * (index + 1) // count]


def load_patches(plan, x_hbm, xp, x_sem, tasks):
    R = plan.R
    cols = 3 * plan.T
    not_first, not_last = edge_masks(plan)
    lanes = [pl.ds(lane, LANES) for lane in range(0, plan.C, LANES)]

    def shift(to, source, by, keep, at, col, _):
        xp[to, col, :, at] = pltpu.roll(xp[source, col, :, at], by, 0) * keep
        return 0

    for i, at in enumerate(lanes):
        patch_copy(x_hbm, xp, x_sem, i).wait()
        lax.fori_loop(0, cols, functools.partial(shift, 0, 3, 1, not_first, at), 0)
        lax.fori_loop(0, cols, functools.partial(shift, 4, 1, R - 1, not_last, at), 0)
        run_all(part_of(tasks, i, len(lanes)))


def patch_copy(x_hbm, xp, x_sem, i):
    at = pl.ds(i * LANES, LANES)
    return pltpu.make_async_copy(x_hbm.at[:, :, :, at], xp.at[pl.ds(1, 3), :, :, at], x_sem.at[i])


def points_kernel(plan, x_hbm, v_hbm, xp, vh, vl, x_sem, v_sem):
    def copies(u):
        return [
            pltpu.make_async_copy(part.at[u], v_hbm.at[which, u], v_sem.at[which, u])
            for which, part in enumerate((vh, vl))
        ]

    for i in range(plan.C // LANES):
        patch_copy(x_hbm, xp, x_sem, i).start()
    load_patches(plan, x_hbm, xp, x_sem, patch_tasks(plan, xp, vh, vl, 0))
    for u in range(5):
        if u > 0:
            run_all(patch_tasks(plan, xp, vh, vl, u))
        for copy in copies(u):
            copy.start()
    for u in range(5):
        for copy in copies(u):
            copy.wait()


def forward_kernel(plan, last, n_refs, tab, mask, bias, *refs):
    refs = list(refs)
    C, N, R, T = plan.C, plan.N, plan.R, plan.T
    cols = 3 * T
    chunks = C // N
    x_hbm = refs.pop(0)
    cot_hbm = refs.pop(0) if last else None
    pieces = [refs.pop(0) for _ in range(n_refs)]
    act_hbm, slope_hbm = refs.pop(0), refs.pop(0)
    if last:
        bias_sum = refs.pop(0)
        outs = [refs.pop(0) for _ in range(plan.n_outs)]
    vh, vl, kbuf, uh, ul, mbuf, ebuf, tail, k_sem, out_sem = refs[:10]
    if last:
        xp, x_sem, cbuf, total, bias_rows, wh, wl, dbuf, c_sem, g_sem, bias_sem = refs[10:]
    else:
        (v_sem,) = refs[10:]

    def cot_copy(n):
        return pltpu.make_async_copy(cot_hbm.at[:, :, :, pl.ds(n * N, N)], cbuf.at[n], c_sem.at[n])

    def v_copies(u):
        return [
            pltpu.make_async_copy(x_hbm.at[which, u], part.at[u], v_sem.at[which, u])
            for which, part in enumerate((vh, vl))
        ]

    def out_copies(n):
        to = pl.ds(n * N, N)
        return [
            pltpu.make_async_copy(ebuf.at[n, pl.ds(0, 3)], act_hbm.at[:, :, :, to], out_sem.at[n, 0]),
            pltpu.make_async_copy(ebuf.at[n, pl.ds(3, 2)], slope_hbm.at[pl.ds(0, 2), :, :, to], out_sem.at[n, 1]),
            pltpu.make_async_copy(tail.at[n], slope_hbm.at[2, :, :, to], out_sem.at[n, 2]),
        ]

    if last:
        patch_copy(x_hbm, xp, x_sem, 0).start()
    else:
        for copy in v_copies(0):
            copy.start()
    start_kernel_fetch(plan, tab, pieces, kbuf.at[0], k_sem.at[0], 0, C, 0, N)
    if last:
        for i in range(1, C // LANES):
            patch_copy(x_hbm, xp, x_sem, i).start()
    else:
        for u in range(1, 5):
            for copy in v_copies(u):
                copy.start()
    for n in range(1, chunks):
        start_kernel_fetch(plan, tab, pieces, kbuf.at[n], k_sem.at[n], 0, C, n * N, N)
    if last:
        for n in range(chunks):
            cot_copy(n).start()
        total[...] = jnp.zeros((16, C), F32)
        load_patches(plan, x_hbm, xp, x_sem, patch_tasks(plan, xp, vh, vl, 0))

    def column_task(s, j, rb):
        n, u = steps[s]
        rows = pl.ds(rb, 16)
        cells = points_to_taps(*[mbuf[s % 2, v, j, rows] for v in range(5)])
        for b in range(3):
            ebuf[n, u, 3 * j + b, rows] = cells[b]

    def column_tasks(s):
        return [functools.partial(column_task, s, j, rb) for j in range(T) for rb in range(0, R, 16)]

    def finish_task(n, col, lane, rb):
        at, rows = pl.ds(lane, LANES), pl.ds(rb, 16)
        wide = pl.ds(n * N + lane, LANES)
        offset = bias[0:1, wide]
        cells = points_to_taps(*[ebuf[n, u, col, rows, at] for u in range(5)])
        sums = None
        for a in range(3):
            value, slope = gelu_parts(cells[a] + offset)
            keep = mask[a, col, rows]
            slope = slope * keep
            if last:
                slope = slope * cbuf[n, a, col, rows, at]
                sums = slope if sums is None else sums + slope
            ebuf[n, a, col, rows, at] = value * keep
            if a < 2:
                ebuf[n, 3 + a, col, rows, at] = slope
            else:
                tail[n, col, rows, at] = slope
        if last:
            total[:, wide] += sums

    def finish_tasks(n):
        return [
            functools.partial(finish_task, n, col, lane, rb)
            for col in range(cols)
            for lane in range(0, N, LANES)
            for rb in range(0, R, 16)
        ]

    steps = [(n, u) for n in range(chunks) for u in range(5)]
    wait_for(kbuf.at[0], k_sem.at[0])
    run_all(tap_tasks(kbuf.at[0], uh.at[0], ul.at[0], 0))
    if last:
        grad = GradSteps(
            plan,
            tab,
            vh,
            vl,
            lambda n: [ebuf.at[n, 3], ebuf.at[n, 4], tail.at[n]],
            wh,
            wl,
            dbuf,
            kbuf,
            False,
            outs,
            g_sem,
        )
    for s, (n, u) in enumerate(steps):
        if u == 4 and n + 1 < chunks:
            wait_for(kbuf.at[n + 1], k_sem.at[n + 1])
            if n == 0 and last:
                for other in range(chunks):
                    cot_copy(other).wait()
        if n == 0 and not last:
            for ready in {0: (0, 1), 2: (2, 3), 4: (4,)}.get(u, ()):
                for copy in v_copies(ready):
                    copy.wait()
        tasks = []
        if s > 0:
            tasks += column_tasks(s - 1)
        if s + 1 < len(steps):
            next_n, next_u = steps[s + 1]
            if n == 0 and u < 4 and last:
                tasks += patch_tasks(plan, xp, vh, vl, u + 1)
            tasks += tap_tasks(kbuf.at[next_n], uh.at[(s + 1) % 2], ul.at[(s + 1) % 2], next_u)
        if n > 0 and u > 0:
            tasks += part_of(finish_tasks(n - 1), u - 1, 4)
        if s + 1 == len(steps) and last:
            if chunks == 1:
                tasks = []
            else:
                tasks += grad.cells(0)

        def put(v, value, s=s):
            mbuf[s % 2, v] = value.reshape(T, R, N)

        interleave(
            dot_tasks(lambda v: (vh[u, v], vl[u, v]), lambda v: (uh[s % 2, v], ul[s % 2, v]), NN, put),
            tasks,
        )
    end = chunks - 1
    if not last:
        for n in range(end):
            for copy in out_copies(n):
                copy.start()
        run_all(column_tasks(len(steps) - 1) + finish_tasks(end))
        for copy in out_copies(end):
            copy.start()
        for n in range(chunks):
            for copy in out_copies(n):
                copy.wait()
        return

    for n in range(end):
        for copy in out_copies(n):
            copy.start()
    closing = column_tasks(len(steps) - 1) + finish_tasks(end)
    if chunks == 1:
        run_all(closing)
        run_all(grad.cells(0))
    for s, (n, u) in enumerate(steps):
        if s + 1 == len(steps) - 3:
            for copy in out_copies(end):
                copy.start()
            for done in range(end):
                grad.store(done)
            bias_rows[...] = jnp.broadcast_to(jnp.sum(total[...], axis=0, keepdims=True), (8, C))
            bias_sum[...] = bias_rows[0:1]
            for copy in bias_copies(plan, bias_rows, outs, bias_sem):
                copy.start()
        tasks = []
        if chunks > 1 and s < 4:
            tasks += part_of(closing, s, 4)
        if s > 0:
            tasks += grad.adds(s - 1)
        if s + 1 < len(steps):
            tasks += grad.cells(s + 1)
        interleave(grad.dots(s), tasks)
    run_all(grad.adds(len(steps) - 1))
    grad.store(end)
    for n in range(chunks):
        for copy in out_copies(n):
            copy.wait()
    for copy in bias_copies(plan, bias_rows, outs, bias_sem):
        copy.wait()
    grad.wait()


def back_kernel(plan, last, n_refs, tab, mask, y_hbm, *refs):
    refs = list(refs)
    C, N, R, T = plan.C, plan.N, plan.R, plan.T
    cols = 3 * T
    chunks = C // N
    if not last:
        slope_hbm, v_hbm = refs.pop(0), refs.pop(0)
    pieces = [refs.pop(0) for _ in range(n_refs)]
    out_hbm = refs.pop(0)
    if not last:
        bias_sum = refs.pop(0)
        outs = [refs.pop(0) for _ in range(plan.n_outs)]
    yb, wh, wl, kbuf, uh, ul, mbuf, ebuf, y_sem, k_sem, out_sem = refs[:11]
    if not last:
        sbuf, total, bias_rows, gh, gl, dbuf, s_sem, v_sem, g_sem, bias_sem = refs[11:]
    lanes = [pl.ds(lane, LANES) for lane in range(0, C, LANES)]

    def y_copy(i):
        return pltpu.make_async_copy(y_hbm.at[:, :, :, lanes[i]], yb.at[:, :, :, lanes[i]], y_sem.at[i])

    def v_copies(u):
        return [
            pltpu.make_async_copy(v_hbm.at[which, u], part.at[u], v_sem.at[which, u])
            for which, part in enumerate((wh, wl))
        ]

    def slope_copy(n):
        return pltpu.make_async_copy(slope_hbm.at[:, :, :, pl.ds(n * N, N)], sbuf.at[n], s_sem.at[n])

    def out_copy(n):
        return pltpu.make_async_copy(ebuf.at[n, pl.ds(0, 3)], out_hbm.at[:, :, :, pl.ds(n * N, N)], out_sem.at[n])

    y_copy(0).start()
    start_kernel_fetch(plan, tab, pieces, kbuf.at[0], k_sem.at[0], 0, N, 0, C)
    for i in range(1, len(lanes)):
        y_copy(i).start()
    for n in range(1, chunks):
        start_kernel_fetch(plan, tab, pieces, kbuf.at[n], k_sem.at[n], n * N, N, 0, C)
    if not last:
        for n in range(chunks):
            slope_copy(n).start()
        total[...] = jnp.zeros((R, C), F32)
    not_first, not_last = edge_masks(plan)
    for parity in range(2):
        for v in (0, 4):
            mbuf[parity, v, 0] = jnp.zeros((R, N), F32)
            mbuf[parity, v, T + 1] = jnp.zeros((R, N), F32)

    def cells(u):
        return cell_tasks(plan, [yb.at[a] for a in range(3)], wh.at[u], wl.at[u], u)

    def column_task(s, j, rb):
        n, u = steps[s]
        rows = pl.ds(rb, 16)
        here = points_to_patch(*[mbuf[s % 2, v, j + 1, rows] for v in range(5)])
        ebuf[n, u, 3 * j, rows] = here[0] + mbuf[s % 2, 4, j, rows]
        ebuf[n, u, 3 * j + 1, rows] = here[1]
        ebuf[n, u, 3 * j + 2, rows] = here[2] + mbuf[s % 2, 0, j + 2, rows]

    def column_tasks(s):
        return [functools.partial(column_task, s, j, rb) for j in range(T) for rb in range(0, R, 16)]

    def finish_task(n, col, lane):
        at = pl.ds(lane, LANES)
        points = [ebuf[n, u, col, :, at] for u in range(5)]
        here = points_to_patch(*points)
        values = (
            here[0] + pltpu.roll(points[4], 1, 0) * not_first,
            here[1],
            here[2] + pltpu.roll(points[0], R - 1, 0) * not_last,
        )
        sums = None
        for a in range(3):
            back = values[a] * (mask[a, col] if last else sbuf[n, a, col, :, at])
            ebuf[n, a, col, :, at] = back
            sums = back if sums is None else sums + back
        if not last:
            total[:, pl.ds(n * N + lane, LANES)] += sums

    def finish_tasks(n):
        return [functools.partial(finish_task, n, col, lane) for col in range(cols) for lane in range(0, N, LANES)]

    first = cells(0)
    for i in range(len(lanes)):
        y_copy(i).wait()
        run_all(part_of(first, i, len(lanes)))
    steps = [(n, u) for n in range(chunks) for u in range(5)]
    wait_for(kbuf.at[0], k_sem.at[0])
    run_all(tap_tasks(kbuf.at[0], uh.at[0], ul.at[0], 0))
    if not last:
        grad = GradSteps(
            plan,
            tab,
            wh,
            wl,
            lambda n: [ebuf.at[n, a] for a in range(3)],
            gh,
            gl,
            dbuf,
            kbuf,
            True,
            outs,
            g_sem,
        )
    for s, (n, u) in enumerate(steps):
        if u == 4 and n + 1 < chunks:
            wait_for(kbuf.at[n + 1], k_sem.at[n + 1])
            if n == 0 and not last:
                for other in range(chunks):
                    slope_copy(other).wait()
        if s == len(steps) - 2 and not last:
            for early in range(3):
                for copy in v_copies(early):
                    copy.start()
        tasks = []
        if s > 0:
            tasks += column_tasks(s - 1)
        if s + 1 < len(steps):
            next_n, next_u = steps[s + 1]
            if n == 0 and u < 4:
                tasks += cells(u + 1)
            tasks += tap_tasks(kbuf.at[next_n], uh.at[(s + 1) % 2], ul.at[(s + 1) % 2], next_u)
        if n > 0 and u > 0:
            tasks += part_of(finish_tasks(n - 1), u - 1, 4)
        if s + 1 == len(steps) and not last and chunks > 1:
            tasks += grad.cells(0)

        def put(v, value, s=s):
            mbuf[s % 2, v, pl.ds(1, T)] = value.reshape(T, R, N)

        interleave(
            dot_tasks(lambda v: (wh[u, v], wl[u, v]), lambda v: (uh[s % 2, v], ul[s % 2, v]), NT, put),
            tasks,
        )
    end = chunks - 1
    for n in range(end):
        out_copy(n).start()
    closing = column_tasks(len(steps) - 1) + finish_tasks(end)
    if last:
        run_all(closing)
        out_copy(end).start()
        for n in range(chunks):
            out_copy(n).wait()
        return

    for late in range(3, 5):
        for copy in v_copies(late):
            copy.start()
    if chunks == 1:
        run_all(closing)
        run_all(grad.cells(0))
    for early in range(3):
        for copy in v_copies(early):
            copy.wait()
    for s, (n, u) in enumerate(steps):
        if s == 2:
            for late in range(3, 5):
                for copy in v_copies(late):
                    copy.wait()
        if s + 1 == len(steps) - 3:
            out_copy(end).start()
            for done in range(end):
                grad.store(done)
            bias_rows[...] = jnp.broadcast_to(jnp.sum(total[...], axis=0, keepdims=True), (8, C))
            bias_sum[...] = bias_rows[0:1]
            for copy in bias_copies(plan, bias_rows, outs, bias_sem):
                copy.start()
        tasks = []
        if chunks > 1 and s < 4:
            tasks += part_of(closing, s, 4)
        if s > 0:
            tasks += grad.adds(s - 1)
        if s + 1 < len(steps):
            tasks += grad.cells(s + 1)
        interleave(grad.dots(s), tasks)
    run_all(grad.adds(len(steps) - 1))
    grad.store(end)
    for n in range(chunks):
        out_copy(n).wait()
    for copy in bias_copies(plan, bias_rows, outs, bias_sem):
        copy.wait()
    grad.wait()


SMEM_SPEC = pl.BlockSpec(memory_space=pltpu.SMEM)
VMEM_SPEC = pl.BlockSpec(memory_space=pltpu.VMEM)
ANY_SPEC = pl.BlockSpec(memory_space=pl.ANY)


def plane_shape(plan):
    return jax.ShapeDtypeStruct((3, 3 * plan.T, plan.R, plan.C), F32)


def point_scratch(plan, width):
    shape = (5, 5, plan.T, plan.R, width)
    return [pltpu.VMEM(shape, BF16), pltpu.VMEM(shape, BF16)]


def call(kernel, outs, in_specs, out_specs, scratch, flops, args, name):
    moved = sum(a.size * a.dtype.itemsize for a in args) + sum(o.size * 4 for o in outs)
    return pl.pallas_call(
        kernel,
        out_shape=outs,
        in_specs=in_specs,
        out_specs=out_specs,
        scratch_shapes=scratch,
        compiler_params=pltpu.CompilerParams(vmem_limit_bytes=VMEM_LIMIT),
        cost_estimate=pl.CostEstimate(flops=flops, bytes_accessed=moved, transcendentals=0),
        name=name,
    )(*args)


def pass_flops(plan):
    return 2 * 3 * 25 * plan.T * plan.R * plan.C * plan.C


def point_shape(plan):
    return jax.ShapeDtypeStruct((2, 5, 5, plan.T, plan.R, plan.C), BF16)


def grad_shapes(plan):
    blocks = 9 * plan.C // plan.block_rows // plan.n_outs
    block = plan.block_rows + (8 if plan.n_outs == 2 else 0)
    return [jax.ShapeDtypeStruct((blocks, block, plan.C), F32) for _ in range(plan.n_outs)]


def grad_scratch(plan):
    shape = (2, 5, plan.T, plan.R, plan.N)
    return [
        pltpu.VMEM((8, plan.C), F32),
        pltpu.VMEM(shape, BF16),
        pltpu.VMEM(shape, BF16),
        pltpu.VMEM((2, 5, plan.C, plan.N), F32),
    ]


def run_points(plan, x, name):
    scratch = [
        pltpu.VMEM((5, 3 * plan.T, plan.R, plan.C), F32),
        *point_scratch(plan, plan.C),
        pltpu.SemaphoreType.DMA((plan.C // LANES,)),
        pltpu.SemaphoreType.DMA((2, 5)),
    ]
    kernel = functools.partial(points_kernel, plan)
    return call(kernel, [point_shape(plan)], [ANY_SPEC], [ANY_SPEC], scratch, x.size * 40, [x], name)[0]


def run_forward(plan, tab, mask, bias, x, cot, pieces, name):
    last = cot is not None
    C, N, R, T = plan.C, plan.N, plan.R, plan.T
    cols = 3 * T
    chunks = C // N
    outs = [plane_shape(plan), plane_shape(plan)]
    scratch = [
        *point_scratch(plan, C),
        pltpu.VMEM((chunks, 9, C, N), F32),
        pltpu.VMEM((2, 5, C, N), BF16),
        pltpu.VMEM((2, 5, C, N), BF16),
        pltpu.VMEM((2, 5, T, R, N), F32),
        pltpu.VMEM((chunks, 5, cols, R, N), F32),
        pltpu.VMEM((chunks, cols, R, N), F32),
        pltpu.SemaphoreType.DMA((chunks,)),
        pltpu.SemaphoreType.DMA((chunks, 3)),
    ]
    args = [tab, mask, bias, x]
    if last:
        outs += [jax.ShapeDtypeStruct((1, C), F32)] + grad_shapes(plan)
        out_specs = [ANY_SPEC, ANY_SPEC, VMEM_SPEC] + [ANY_SPEC] * plan.n_outs
        scratch += [
            pltpu.VMEM((5, cols, R, C), F32),
            pltpu.SemaphoreType.DMA((C // LANES,)),
            pltpu.VMEM((chunks, 3, cols, R, N), F32),
            pltpu.VMEM((16, C), F32),
            *grad_scratch(plan),
            pltpu.SemaphoreType.DMA((chunks,)),
            pltpu.SemaphoreType.DMA((chunks,)),
            pltpu.SemaphoreType.DMA,
        ]
        args.append(cot)
    else:
        out_specs = [ANY_SPEC] * 2
        scratch.append(pltpu.SemaphoreType.DMA((2, 5)))
    args += pieces
    in_specs = [SMEM_SPEC, VMEM_SPEC, VMEM_SPEC] + [ANY_SPEC] * (len(args) - 3)
    kernel = functools.partial(forward_kernel, plan, last, len(pieces))
    return call(kernel, outs, in_specs, out_specs, scratch, pass_flops(plan) * (1 + last), args, name)


def run_back(plan, tab, mask, y, slope, points, pieces, name):
    last = slope is None
    C, N, R, T = plan.C, plan.N, plan.R, plan.T
    cols = 3 * T
    chunks = C // N
    outs = [plane_shape(plan)]
    out_specs = [ANY_SPEC]
    scratch = [
        pltpu.VMEM((3, cols, R, C), F32),
        *point_scratch(plan, C),
        pltpu.VMEM((chunks, 9, N, C), F32),
        pltpu.VMEM((2, 5, N, C), BF16),
        pltpu.VMEM((2, 5, N, C), BF16),
        pltpu.VMEM((2, 5, T + 2, R, N), F32),
        pltpu.VMEM((chunks, 5, cols, R, N), F32),
        pltpu.SemaphoreType.DMA((C // LANES,)),
        pltpu.SemaphoreType.DMA((chunks,)),
        pltpu.SemaphoreType.DMA((chunks,)),
    ]
    args = [tab, mask, y]
    if not last:
        outs += [jax.ShapeDtypeStruct((1, C), F32)] + grad_shapes(plan)
        out_specs += [VMEM_SPEC] + [ANY_SPEC] * plan.n_outs
        scratch += [
            pltpu.VMEM((chunks, 3, cols, R, N), F32),
            pltpu.VMEM((R, C), F32),
            *grad_scratch(plan),
            pltpu.SemaphoreType.DMA((chunks,)),
            pltpu.SemaphoreType.DMA((2, 5)),
            pltpu.SemaphoreType.DMA((chunks,)),
            pltpu.SemaphoreType.DMA,
        ]
        args += [slope, points]
    args += pieces
    mask_spec = VMEM_SPEC if last else ANY_SPEC
    in_specs = [SMEM_SPEC, mask_spec] + [ANY_SPEC] * (len(args) - 2)
    kernel = functools.partial(back_kernel, plan, last, len(pieces))
    return call(kernel, outs, in_specs, out_specs, scratch, pass_flops(plan) * (2 - last), args, name)


def to_planes(plan, cells):
    slots, side, _, channels = cells.shape
    tiled = cells.reshape(slots, plan.T, 3, side, channels).transpose(2, 3, 0, 1, 4)
    flat = tiled.reshape(3, side, slots * plan.T, channels)
    return jnp.pad(flat, ((0, 0), (0, 0), (0, plan.R - slots * plan.T), (0, 0)))


def from_planes(plan, planes, slots):
    side = 3 * plan.T
    kept = planes[:, :, : slots * plan.T].reshape(3, side, slots, plan.T, planes.shape[3])
    return kept.transpose(2, 3, 0, 1, 4).reshape(slots, side, side, planes.shape[3])


def tie(*values):
    return lax.optimization_barrier(values)


class Net:
    def __init__(self):
        self.rep = lax.axis_size("rep")
        self.dp = lax.axis_size("dp")
        self.routed = self.rep == 4 and self.dp == 8
        self.n_pieces = 4 if self.routed else 1
        self.n_outs = 2 if self.routed else 1

    def perm(self, move):
        pairs = []
        for x in range(2):
            for c in range(2):
                for z in range(4):
                    for y in range(2):
                        to = move(x, c, z, y)
                        pairs.append((((x * 2 + c) * 4 + z) * 2 + y, ((to[0] * 2 + to[1]) * 4 + to[2]) * 2 + to[3]))
        return pairs

    def send(self, value, move):
        return lax.ppermute(value, AXES, self.perm(move))

    def over_core(self, value):
        return self.send(value, lambda x, c, z, y: (x, 1 - c, z, y))

    def over_first(self, value):
        return self.send(value, lambda x, c, z, y: (x, c, z, 1 - y) if c == 0 else (1 - x, c, z, y))

    def over_second(self, value):
        return self.send(value, lambda x, c, z, y: (1 - x, c, z, y) if c == 0 else (x, c, z, 1 - y))

    def over_both(self, value):
        return self.send(value, lambda x, c, z, y: (1 - x, c, z, 1 - y))

    def over_z(self, value, step):
        return self.send(value, lambda x, c, z, y: (x, c, (z + step) % 4, y))

    def tables(self):
        if not self.routed:
            return jnp.zeros((4, 8), jnp.int32)
        rep = lax.axis_index("rep")
        dp = lax.axis_index("dp")
        x, c, z, y = rep // 2, rep % 2, dp // 2, dp % 2
        block = jnp.arange(32, dtype=jnp.int32)
        bx, bc, bz, by = block // 16, block // 8 % 2, block // 2 % 4, block % 2
        dx, dy = bx ^ x, by ^ y
        second = jnp.where(bc == 0, dx, dy)
        first = jnp.where(bc == 0, dy, dx)
        other = (bc != c).astype(jnp.int32)
        return jnp.stack(
            [2 * other + second, 4 * first + (z - bz) % 4, other, 8 * second + 4 * first + (bz - z) % 4]
        ).astype(jnp.int32)

    def gather_z(self, shard):
        return jnp.stack([shard] + [self.over_z(shard, step) for step in (1, 2, 3)])

    def double(self, part):
        return jnp.concatenate([part, self.over_first(part)])

    def gather_whole(self, shard):
        return [lax.all_gather(shard, AXES, axis=0, tiled=True)[None]]

    def sum_whole(self, parts):
        return lax.psum_scatter(parts[0][0], AXES, scatter_dimension=0, tiled=True)

    def send_z(self, four):
        return [four[0]] + [self.over_z(four[step], step) for step in (1, 2, 3)]


def body(
    features, map_size, item_count, conv4_weight, conv4_bias, conv5_weight, conv5_bias, cotangent
):
    slots, side, _, channels = features.shape
    net = Net()
    tiles = side // 3
    rows = -(-slots * tiles // 16) * 16
    shard_rows = conv4_weight.shape[0] // channels
    block_rows = shard_rows if net.routed else 9 * channels
    plan = Plan(channels, rows, tiles, block_rows, net.n_pieces, net.n_outs)

    live = jnp.arange(slots, dtype=jnp.int32) < item_count[0]
    inside = jnp.arange(side, dtype=jnp.int32)[None, :] < map_size[:, None]
    valid = live[:, None, None] & inside[:, :, None] & inside[:, None, :]
    mask = to_planes(plan, jnp.broadcast_to(valid.astype(F32)[..., None], (slots, side, side, LANES)))
    source = to_planes(plan, features * valid.astype(F32)[..., None])
    cot = to_planes(plan, cotangent)
    tab = net.tables()

    shard4 = conv4_weight.reshape(shard_rows, channels)
    shard5 = conv5_weight.reshape(shard_rows, channels)
    if net.routed:
        four4 = net.gather_z(shard4)
        shard5, four4, source, mask, cot = tie(shard5, four4, source, mask, cot)
        four5 = net.gather_z(shard5)
        eight4 = net.double(four4)
        far4 = net.over_second(eight4)
        four5, far4, eight4 = tie(four5, far4, eight4)
        points4 = run_points(plan, source, "points4")
        pieces4 = [eight4, far4, net.over_core(eight4), net.over_core(far4)]
        eight5 = net.double(four5)
        eight5, points4 = tie(eight5, points4)
        far5 = net.over_second(eight5)
        near5 = net.over_core(eight5)
    else:
        pieces4 = net.gather_whole(shard4)
        pieces5 = net.gather_whole(shard5)
        points4 = run_points(plan, source, "points4")
    hidden, slope4 = run_forward(plan, tab, mask, conv4_bias[None], points4, None, pieces4, "conv4")
    if net.routed:
        far5, near5, hidden = tie(far5, near5, hidden)
        pieces5 = [eight5, far5, near5, net.over_core(far5)]
    out5, back5, bias5, *grad5 = run_forward(
        plan, tab, mask, conv5_bias[None], hidden, cot, pieces5, "conv5_grad5"
    )
    if net.routed:
        mine5, other5 = grad5
        core5 = net.over_core(other5)
        sends5 = [mine5[i : i + 4] + core5[i : i + 4] for i in (4, 8, 12)]
        *sends5, back5 = tie(*sends5, back5)
        got5 = [net.over_first(sends5[0]), net.over_second(sends5[1]), net.over_both(sends5[2])]
    back4, bias4, *grad4 = run_back(plan, tab, mask, back5, slope4, points4, pieces5, "back5_grad4")
    if net.routed:
        mine4, theirs4 = grad4
        core4, *got5 = tie(net.over_core(theirs4), *got5)
        four5 = mine5[:4] + core5[:4] + got5[0] + got5[1] + got5[2]
        send4, four5, back4 = tie(mine4[8:] + core4[8:], four5, back4)
        second4 = net.over_second(send4)
        got5 = net.send_z(four5)
    input_grad = run_back(plan, tab, mask, back4, None, None, pieces4, "back4")[0]
    if net.routed:
        second4, input_grad, *got5 = tie(second4, input_grad, *got5)
        first4 = net.over_first(mine4[4:8] + core4[4:8] + second4[4:])
        sum4 = sum(net.send_z(mine4[:4] + core4[:4] + second4[:4] + first4))
        sum5 = sum(got5)
        share4, total4 = sum4[:shard_rows], sum4[shard_rows]
        share5, total5 = sum5[:shard_rows], sum5[shard_rows]
    else:
        share5 = net.sum_whole(grad5)
        share4 = net.sum_whole(grad4)
        total4, total5 = lax.psum((bias4[0], bias5[0]), AXES)

    total_cells = slots * net.rep * net.dp * side * side
    scale = float(total_cells) ** (-0.5)
    return (
        from_planes(plan, out5, slots),
        from_planes(plan, input_grad, slots),
        (share4 * scale).reshape(-1),
        total4 * scale,
        (share5 * scale).reshape(-1),
        total5 * scale,
    )


def solution(mesh):
    placed = (
        P(AXES, None, None, None),
        P(AXES),
        P(AXES),
        P(AXES),
        P(),
        P(AXES),
        P(),
        P(AXES, None, None, None),
    )
    return jax.shard_map(
        body,
        mesh=mesh,
        in_specs=placed,
        out_specs=(
            P(AXES, None, None, None),
            P(AXES, None, None, None),
            P(AXES),
            P(),
            P(AXES),
            P(),
        ),
        check_vma=False,
    )
```

```python
import functools

import jax
import jax.numpy as jnp
from jax import lax
from jax.experimental import pallas as pl
from jax.experimental.pallas import tpu as pltpu
from jax.sharding import PartitionSpec as P

AXES = ("rep", "dp")
F32 = jnp.float32
BF16 = jnp.bfloat16
LANES = 128
VMEM_LIMIT = 62 * 2**20
NN = (((1,), (0,)), ((), ()))
NT = (((1,), (1,)), ((), ()))
TN = (((0,), (0,)), ((), ()))
GELU_K = 0.7978845608028654
GELU_C = 0.044715


def patch_to_points(p0, p1, p2, p3, p4):
    d = p3 - p1
    return (
        (p0 - p2) + 0.5 * d,
        p1 + 0.5 * (p2 - p3),
        0.5 * p2 - (1.0 / 6.0) * (p1 + p1 + p3),
        (1.0 / 6.0) * d,
        (p4 - p2) - 2.0 * d,
    )


def points_to_patch(n0, n1, n2, n3, n4):
    e = 0.5 * n0 - 2.0 * n4
    f = (1.0 / 6.0) * n3
    g = (1.0 / 6.0) * n2
    return (
        (n1 - e) - (g + g + f),
        0.5 * (n1 + n2) - (n0 + n4),
        (e - 0.5 * n1) + (f - g),
    )


def taps_to_points(k0, k1, k2):
    s = k0 + k2
    return (k0, s + k1, s - k1, k0 + 2.0 * (k1 + 2.0 * k2), k2)


def taps_to_point(index, k0, k1, k2, at):
    if index == 0:
        return k0[at]
    if index == 1:
        return (k0[at] + k2[at]) + k1[at]
    if index == 2:
        return (k0[at] + k2[at]) - k1[at]
    if index == 3:
        return k0[at] + 2.0 * (k1[at] + 2.0 * k2[at])
    return k2[at]


POINT_TAPS = (((0, 1.0),), ((0, 1.0), (1, 1.0), (2, 1.0)), ((0, 1.0), (1, -1.0), (2, 1.0)), ((0, 1.0), (1, 2.0), (2, 4.0)), ((2, 1.0),))


def points_to_taps(d0, d1, d2, d3, d4):
    s = d1 + d2
    return (d0 + s + d3, (d1 - d2) + 2.0 * d3, s + 4.0 * d3 + d4)


def split(value):
    high = value.astype(BF16)
    return high, (value - high.astype(F32)).astype(BF16)


def dot3(left_high, left_low, right_high, right_low, dims):
    def dot(left, right):
        return lax.dot_general(left, right, dims, preferred_element_type=F32)

    return dot(left_high, right_high) + dot(left_low, right_high) + dot(left_high, right_low)


def gelu_parts(v):
    square = v * v
    half = 0.5 + 0.5 * jnp.tanh(v * (GELU_K + (GELU_K * GELU_C) * square))
    value = v * half
    return value, half + value * ((1.0 - half) * (2.0 * GELU_K + (6.0 * GELU_K * GELU_C) * square))


def segments(tap, start, rows, tap_rows, block_rows):
    cuts = []
    at = tap * tap_rows + start
    end = at + rows
    first = at
    while at < end:
        block = at // block_rows
        stop = min(end, (block + 1) * block_rows)
        cuts.append((block, at - block * block_rows, at - first, stop - at))
        at = stop
    return cuts


class Plan:
    def __init__(self, channels, rows, tiles, block_rows, n_pieces, n_outs):
        self.C = channels
        self.R = rows
        self.T = tiles
        self.block_rows = block_rows
        self.n_pieces = n_pieces
        self.n_outs = n_outs
        self.N = min(256, channels)


def for_each_cut(plan, tab, row, count, cut_block, act):
    if count == 1:
        act(0, 0)
        return
    which = tab[row, cut_block]
    index = tab[row + 1, cut_block]
    for ref in range(count):
        pl.when(which == ref)(functools.partial(act, ref, index))


def start_kernel_fetch(plan, tab, pieces, buf, sem, row_start, rows, col_start, cols, taps=range(9)):
    for first in range(0, len(pieces), plan.n_pieces):
        group = pieces[first : first + plan.n_pieces]
        width = group[0].shape[2]
        group_start = first // plan.n_pieces * width
        low = max(col_start, group_start)
        high = min(col_start + cols, group_start + width)
        if low >= high:
            continue
        for tap in taps:
            for block, at, to, length in segments(tap, row_start, rows, plan.C, plan.block_rows):

                def act(ref, index, tap=tap, at=at, to=to, length=length):
                    pltpu.make_async_copy(
                        group[ref].at[index, pl.ds(at, length), pl.ds(low - group_start, high - low)],
                        buf.at[tap, pl.ds(to, length), pl.ds(low - col_start, high - low)],
                        sem,
                    ).start()

                for_each_cut(plan, tab, 0, plan.n_pieces, block, act)


def start_grad_store(plan, tab, buf, folded, outs, sem, col_start):
    N = plan.N
    for tap in range(9):
        for start in range(0, plan.C, N):
            for block, at, to, length in segments(tap, start, N, plan.C, plan.block_rows):
                if folded:
                    part = buf.at[tap, pl.ds(to, length), pl.ds(start, N)]
                else:
                    part = buf.at[tap, pl.ds(start + to, length)]

                def act(ref, index, part=part, at=at, length=length):
                    pltpu.make_async_copy(
                        part, outs[ref].at[index, pl.ds(at, length), pl.ds(col_start, N)], sem
                    ).start()

                for_each_cut(plan, tab, 2, plan.n_outs, block, act)


def wait_for(buf, sem):
    pltpu.make_async_copy(buf, buf, sem).wait()


def edge_masks(plan):
    place = lax.broadcasted_iota(jnp.int32, (plan.R, LANES), 0) % plan.T
    return (place != 0).astype(F32), (place != plan.T - 1).astype(F32)


def interleave(dots, tasks):
    done = 0
    for i, dot in enumerate(dots):
        dot()
        upto = len(tasks) * (i + 1) // len(dots)
        for task in tasks[done:upto]:
            task()
        done = upto


def run_all(tasks):
    for task in tasks:
        task()


def store_split(high_ref, low_ref, at, value):
    high, low = split(value)
    high_ref[at] = high
    low_ref[at] = low


def patch_tasks(plan, xp, vh, vl, u):
    T = plan.T

    def task(lane, rb):
        rows, at = pl.ds(rb, 16), pl.ds(lane, LANES)
        line = []
        for col in range(3 * T + 2):
            if col in (0, 3 * T + 1):
                line.append(jnp.zeros((16, LANES), F32))
            else:
                line.append(patch_to_point(u, [xp.at[k, col - 1] for k in range(5)], (rows, at)))
        for j in range(T):
            for v, value in enumerate(patch_to_points(*line[3 * j : 3 * j + 5])):
                store_split(vh, vl, (u, v, j, rows, at), value)

    return [functools.partial(task, lane, rb) for lane in range(0, plan.C, LANES) for rb in range(0, plan.R, 16)]


def patch_to_point(u, planes, at):
    if u == 0:
        return (planes[0][at] - planes[2][at]) + 0.5 * (planes[3][at] - planes[1][at])
    if u == 1:
        return planes[1][at] + 0.5 * (planes[2][at] - planes[3][at])
    if u == 2:
        p1 = planes[1][at]
        return 0.5 * planes[2][at] - (1.0 / 6.0) * (p1 + p1 + planes[3][at])
    if u == 3:
        return (1.0 / 6.0) * (planes[3][at] - planes[1][at])
    return (planes[4][at] - planes[2][at]) - 2.0 * (planes[3][at] - planes[1][at])


def cell_tasks(plan, planes, wh, wl, u):
    def task(lane, j, rb):
        rows, at = pl.ds(rb, 16), pl.ds(lane, LANES)
        line = [taps_to_point(u, *[plane.at[3 * j + b] for plane in planes], (rows, at)) for b in range(3)]
        for v, value in enumerate(taps_to_points(*line)):
            store_split(wh, wl, (v, j, rows, at), value)

    return [
        functools.partial(task, lane, j, rb)
        for lane in range(0, planes[0].shape[2], LANES)
        for j in range(plan.T)
        for rb in range(0, plan.R, 16)
    ]


def tap_tasks(kbuf, uh, ul, point):
    def task(row):
        at = pl.ds(row, 16)
        parts = [taps_to_point(point, kbuf.at[q], kbuf.at[3 + q], kbuf.at[6 + q], at) for q in range(3)]
        for v, value in enumerate(taps_to_points(*parts)):
            store_split(uh, ul, (v, at), value)

    return [functools.partial(task, row) for row in range(0, kbuf.shape[1], 16)]


def dot_tasks(lefts, rights, dims, put):
    def dot(v):
        left = tuple(part.reshape(part.shape[0] * part.shape[1], part.shape[2]) for part in lefts(v))
        put(v, dot3(*left, *rights(v), dims))

    return [functools.partial(dot, v) for v in range(5)]


class GradSteps:
    def __init__(self, plan, tab, vh, vl, planes_of, wh, wl, dbuf, grads, folded, outs, out_sem):
        self.plan, self.tab, self.vh, self.vl, self.planes_of = plan, tab, vh, vl, planes_of
        self.wh, self.wl, self.dbuf, self.grads, self.folded = wh, wl, dbuf, grads, folded
        self.outs, self.out_sem = outs, out_sem
        self.steps = [(n, u) for n in range(plan.C // plan.N) for u in range(5)]

    def cells(self, s):
        n, u = self.steps[s]
        return cell_tasks(self.plan, self.planes_of(n), self.wh.at[s % 2], self.wl.at[s % 2], u)

    def add(self, s, row):
        n, u = self.steps[s]
        plan, grad = self.plan, self.grads.at[n]
        taps = points_to_taps(*[self.dbuf[s % 2, v, pl.ds(row, 16)] for v in range(5)])
        if self.folded:
            place = (pl.ds(row % plan.N, 16), pl.ds(row // plan.N * plan.N, plan.N))
        else:
            place = (pl.ds(row, 16), slice(None))
        for k, weight in POINT_TAPS[u]:
            for q in range(3):
                term = taps[q] if weight == 1.0 else weight * taps[q]
                if u == 0 or (u == 1 and k > 0):
                    grad[(3 * k + q, *place)] = term
                else:
                    grad[(3 * k + q, *place)] += term

    def adds(self, s):
        return [functools.partial(self.add, s, row) for row in range(0, self.plan.C, 16)]

    def dots(self, s):
        n, u = self.steps[s]
        rows = self.plan.T * self.plan.R

        def put(v, value):
            self.dbuf[s % 2, v] = value

        def rights(v):
            return tuple(part[s % 2, v].reshape(rows, self.plan.N) for part in (self.wh, self.wl))

        return dot_tasks(lambda v: (self.vh[u, v], self.vl[u, v]), rights, TN, put)

    def store(self, n):
        start_grad_store(
            self.plan, self.tab, self.grads.at[n], self.folded, self.outs, self.out_sem.at[n], n * self.plan.N
        )

    def wait(self):
        for n in range(self.plan.C // self.plan.N):
            wait_for(self.grads.at[n], self.out_sem.at[n])


def bias_copies(plan, rows, outs, sem):
    if plan.n_outs == 1:
        return []
    return [
        pltpu.make_async_copy(rows, out.at[i, pl.ds(plan.block_rows, 8)], sem)
        for out in outs
        for i in range(out.shape[0])
    ]


def part_of(tasks, index, count):
    return tasks[len(tasks) * index // count : len(tasks) * (index + 1) // count]


def load_patches(plan, x_hbm, xp, x_sem, tasks):
    R = plan.R
    cols = 3 * plan.T
    not_first, not_last = edge_masks(plan)
    lanes = [pl.ds(lane, LANES) for lane in range(0, plan.C, LANES)]

    def shift(to, source, by, keep, at, col, _):
        xp[to, col, :, at] = pltpu.roll(xp[source, col, :, at], by, 0) * keep
        return 0

    for i, at in enumerate(lanes):
        patch_copy(x_hbm, xp, x_sem, i).wait()
        lax.fori_loop(0, cols, functools.partial(shift, 0, 3, 1, not_first, at), 0)
        lax.fori_loop(0, cols, functools.partial(shift, 4, 1, R - 1, not_last, at), 0)
        run_all(part_of(tasks, i, len(lanes)))


def patch_copy(x_hbm, xp, x_sem, i):
    at = pl.ds(i * LANES, LANES)
    return pltpu.make_async_copy(x_hbm.at[:, :, :, at], xp.at[pl.ds(1, 3), :, :, at], x_sem.at[i])


def points_kernel(plan, x_hbm, v_hbm, xp, vh, vl, x_sem, v_sem):
    def copies(u):
        return [
            pltpu.make_async_copy(part.at[u], v_hbm.at[which, u], v_sem.at[which, u])
            for which, part in enumerate((vh, vl))
        ]

    for i in range(plan.C // LANES):
        patch_copy(x_hbm, xp, x_sem, i).start()
    load_patches(plan, x_hbm, xp, x_sem, patch_tasks(plan, xp, vh, vl, 0))
    for u in range(5):
        if u > 0:
            run_all(patch_tasks(plan, xp, vh, vl, u))
        for copy in copies(u):
            copy.start()
    for u in range(5):
        for copy in copies(u):
            copy.wait()


def forward_kernel(plan, last, n_refs, tab, mask, bias, *refs):
    refs = list(refs)
    C, N, R, T = plan.C, plan.N, plan.R, plan.T
    cols = 3 * T
    chunks = C // N
    x_hbm = refs.pop(0)
    cot_hbm = refs.pop(0) if last else None
    pieces = [refs.pop(0) for _ in range(n_refs)]
    act_hbm, slope_hbm = refs.pop(0), refs.pop(0)
    if last:
        bias_sum = refs.pop(0)
        outs = [refs.pop(0) for _ in range(plan.n_outs)]
    vh, vl, kbuf, uh, ul, mbuf, ebuf, tail, k_sem, out_sem = refs[:10]
    if last:
        xp, x_sem, cbuf, total, bias_rows, wh, wl, dbuf, c_sem, g_sem, bias_sem = refs[10:]
    else:
        (v_sem,) = refs[10:]

    def cot_copy(n):
        return pltpu.make_async_copy(cot_hbm.at[:, :, :, pl.ds(n * N, N)], cbuf.at[n], c_sem.at[n])

    def v_copies(u):
        return [
            pltpu.make_async_copy(x_hbm.at[which, u], part.at[u], v_sem.at[which, u])
            for which, part in enumerate((vh, vl))
        ]

    def out_copies(n):
        to = pl.ds(n * N, N)
        return [
            pltpu.make_async_copy(ebuf.at[n, pl.ds(0, 3)], act_hbm.at[:, :, :, to], out_sem.at[n, 0]),
            pltpu.make_async_copy(ebuf.at[n, pl.ds(3, 2)], slope_hbm.at[pl.ds(0, 2), :, :, to], out_sem.at[n, 1]),
            pltpu.make_async_copy(tail.at[n], slope_hbm.at[2, :, :, to], out_sem.at[n, 2]),
        ]

    if last:
        for i in range(C // LANES):
            patch_copy(x_hbm, xp, x_sem, i).start()
    else:
        for copy in v_copies(0):
            copy.start()
    start_kernel_fetch(plan, tab, pieces, kbuf.at[0], k_sem.at[chunks], 0, C, 0, N, range(3))
    start_kernel_fetch(plan, tab, pieces, kbuf.at[0], k_sem.at[0], 0, C, 0, N, range(3, 9))
    if not last:
        for u in range(1, 5):
            for copy in v_copies(u):
                copy.start()
    for n in range(1, chunks):
        start_kernel_fetch(plan, tab, pieces, kbuf.at[n], k_sem.at[n], 0, C, n * N, N)
    if last:
        for n in range(chunks):
            cot_copy(n).start()
        total[...] = jnp.zeros((16, C), F32)
        load_patches(plan, x_hbm, xp, x_sem, patch_tasks(plan, xp, vh, vl, 0))

    def column_task(s, j, rb):
        n, u = steps[s]
        rows = pl.ds(rb, 16)
        cells = points_to_taps(*[mbuf[s % 2, v, j, rows] for v in range(5)])
        for b in range(3):
            ebuf[n, u, 3 * j + b, rows] = cells[b]

    def column_tasks(s):
        return [functools.partial(column_task, s, j, rb) for j in range(T) for rb in range(0, R, 16)]

    def finish_task(n, col, lane, rb):
        at, rows = pl.ds(lane, LANES), pl.ds(rb, 16)
        wide = pl.ds(n * N + lane, LANES)
        offset = bias[0:1, wide]
        cells = points_to_taps(*[ebuf[n, u, col, rows, at] for u in range(5)])
        sums = None
        for a in range(3):
            value, slope = gelu_parts(cells[a] + offset)
            keep = mask[a, col, rows]
            slope = slope * keep
            if last:
                slope = slope * cbuf[n, a, col, rows, at]
                sums = slope if sums is None else sums + slope
            ebuf[n, a, col, rows, at] = value * keep
            if a < 2:
                ebuf[n, 3 + a, col, rows, at] = slope
            else:
                tail[n, col, rows, at] = slope
        if last:
            total[:, wide] += sums

    def finish_tasks(n):
        return [
            functools.partial(finish_task, n, col, lane, rb)
            for col in range(cols)
            for lane in range(0, N, LANES)
            for rb in range(0, R, 16)
        ]

    steps = [(n, u) for n in range(chunks) for u in range(5)]
    wait_for(kbuf.at[0, pl.ds(0, 3)], k_sem.at[chunks])
    run_all(tap_tasks(kbuf.at[0], uh.at[0], ul.at[0], 0))
    if last:
        grad = GradSteps(
            plan,
            tab,
            vh,
            vl,
            lambda n: [ebuf.at[n, 3], ebuf.at[n, 4], tail.at[n]],
            wh,
            wl,
            dbuf,
            kbuf,
            False,
            outs,
            g_sem,
        )
    for s, (n, u) in enumerate(steps):
        if s == 0:
            wait_for(kbuf.at[0, pl.ds(3, 6)], k_sem.at[0])
        if u == 4 and n + 1 < chunks:
            wait_for(kbuf.at[n + 1], k_sem.at[n + 1])
            if n == 0 and last:
                for other in range(chunks):
                    cot_copy(other).wait()
        if n == 0 and not last:
            for ready in {0: (0, 1), 2: (2, 3), 4: (4,)}.get(u, ()):
                for copy in v_copies(ready):
                    copy.wait()
        tasks = []
        if s > 0:
            tasks += column_tasks(s - 1)
        if s + 1 < len(steps):
            next_n, next_u = steps[s + 1]
            if n == 0 and u < 4 and last:
                tasks += patch_tasks(plan, xp, vh, vl, u + 1)
            tasks += tap_tasks(kbuf.at[next_n], uh.at[(s + 1) % 2], ul.at[(s + 1) % 2], next_u)
        if n > 0 and u > 0:
            tasks += part_of(finish_tasks(n - 1), u - 1, 4)
        if s + 1 == len(steps) and last:
            if chunks == 1:
                tasks = []
            else:
                tasks += grad.cells(0)

        def put(v, value, s=s):
            mbuf[s % 2, v] = value.reshape(T, R, N)

        interleave(
            dot_tasks(lambda v: (vh[u, v], vl[u, v]), lambda v: (uh[s % 2, v], ul[s % 2, v]), NN, put),
            tasks,
        )
    end = chunks - 1
    if not last:
        for n in range(end):
            for copy in out_copies(n):
                copy.start()
        run_all(column_tasks(len(steps) - 1) + finish_tasks(end))
        for copy in out_copies(end):
            copy.start()
        for n in range(chunks):
            for copy in out_copies(n):
                copy.wait()
        return

    for n in range(end):
        for copy in out_copies(n):
            copy.start()
    closing = column_tasks(len(steps) - 1) + finish_tasks(end)
    if chunks == 1:
        run_all(closing)
        run_all(grad.cells(0))
    for s, (n, u) in enumerate(steps):
        if s + 1 == len(steps) - 3:
            for copy in out_copies(end):
                copy.start()
            for done in range(end):
                grad.store(done)
            bias_rows[...] = jnp.broadcast_to(jnp.sum(total[...], axis=0, keepdims=True), (8, C))
            bias_sum[...] = bias_rows[0:1]
            for copy in bias_copies(plan, bias_rows, outs, bias_sem):
                copy.start()
        tasks = []
        if chunks > 1 and s < 4:
            tasks += part_of(closing, s, 4)
        if s > 0:
            tasks += grad.adds(s - 1)
        if s + 1 < len(steps):
            tasks += grad.cells(s + 1)
        interleave(grad.dots(s), tasks)
    run_all(grad.adds(len(steps) - 1))
    grad.store(end)
    for n in range(chunks):
        for copy in out_copies(n):
            copy.wait()
    for copy in bias_copies(plan, bias_rows, outs, bias_sem):
        copy.wait()
    grad.wait()


def back_kernel(plan, last, n_refs, tab, mask, y_hbm, *refs):
    refs = list(refs)
    C, N, R, T = plan.C, plan.N, plan.R, plan.T
    cols = 3 * T
    chunks = C // N
    if not last:
        slope_hbm, v_hbm = refs.pop(0), refs.pop(0)
    pieces = [refs.pop(0) for _ in range(n_refs)]
    out_hbm = refs.pop(0)
    if not last:
        bias_sum = refs.pop(0)
        outs = [refs.pop(0) for _ in range(plan.n_outs)]
    yb, wh, wl, kbuf, uh, ul, mbuf, ebuf, y_sem, k_sem, out_sem = refs[:11]
    if not last:
        sbuf, total, bias_rows, gh, gl, dbuf, s_sem, v_sem, g_sem, bias_sem = refs[11:]
    lanes = [pl.ds(lane, LANES) for lane in range(0, C, LANES)]

    def y_copy(i):
        return pltpu.make_async_copy(y_hbm.at[:, :, :, lanes[i]], yb.at[:, :, :, lanes[i]], y_sem.at[i])

    def v_copies(u):
        return [
            pltpu.make_async_copy(v_hbm.at[which, u], part.at[u], v_sem.at[which, u])
            for which, part in enumerate((wh, wl))
        ]

    def slope_copy(n):
        return pltpu.make_async_copy(slope_hbm.at[:, :, :, pl.ds(n * N, N)], sbuf.at[n], s_sem.at[n])

    def out_copy(n):
        return pltpu.make_async_copy(ebuf.at[n, pl.ds(0, 3)], out_hbm.at[:, :, :, pl.ds(n * N, N)], out_sem.at[n])

    for i in range(len(lanes)):
        y_copy(i).start()
    start_kernel_fetch(plan, tab, pieces, kbuf.at[0], k_sem.at[chunks], 0, N, 0, C, range(3))
    start_kernel_fetch(plan, tab, pieces, kbuf.at[0], k_sem.at[0], 0, N, 0, C, range(3, 9))
    for n in range(1, chunks):
        start_kernel_fetch(plan, tab, pieces, kbuf.at[n], k_sem.at[n], n * N, N, 0, C)
    if not last:
        for n in range(chunks):
            slope_copy(n).start()
        total[...] = jnp.zeros((R, C), F32)
    not_first, not_last = edge_masks(plan)
    for parity in range(2):
        for v in (0, 4):
            mbuf[parity, v, 0] = jnp.zeros((R, N), F32)
            mbuf[parity, v, T + 1] = jnp.zeros((R, N), F32)

    def cells(u):
        return cell_tasks(plan, [yb.at[a] for a in range(3)], wh.at[u], wl.at[u], u)

    def column_task(s, j, rb):
        n, u = steps[s]
        rows = pl.ds(rb, 16)
        here = points_to_patch(*[mbuf[s % 2, v, j + 1, rows] for v in range(5)])
        ebuf[n, u, 3 * j, rows] = here[0] + mbuf[s % 2, 4, j, rows]
        ebuf[n, u, 3 * j + 1, rows] = here[1]
        ebuf[n, u, 3 * j + 2, rows] = here[2] + mbuf[s % 2, 0, j + 2, rows]

    def column_tasks(s):
        return [functools.partial(column_task, s, j, rb) for j in range(T) for rb in range(0, R, 16)]

    def finish_task(n, col, lane):
        at = pl.ds(lane, LANES)
        points = [ebuf[n, u, col, :, at] for u in range(5)]
        here = points_to_patch(*points)
        values = (
            here[0] + pltpu.roll(points[4], 1, 0) * not_first,
            here[1],
            here[2] + pltpu.roll(points[0], R - 1, 0) * not_last,
        )
        sums = None
        for a in range(3):
            back = values[a] * (mask[a, col] if last else sbuf[n, a, col, :, at])
            ebuf[n, a, col, :, at] = back
            sums = back if sums is None else sums + back
        if not last:
            total[:, pl.ds(n * N + lane, LANES)] += sums

    def finish_tasks(n):
        return [functools.partial(finish_task, n, col, lane) for col in range(cols) for lane in range(0, N, LANES)]

    first = cells(0)
    for i in range(len(lanes)):
        y_copy(i).wait()
        run_all(part_of(first, i, len(lanes)))
    steps = [(n, u) for n in range(chunks) for u in range(5)]
    wait_for(kbuf.at[0, pl.ds(0, 3)], k_sem.at[chunks])
    run_all(tap_tasks(kbuf.at[0], uh.at[0], ul.at[0], 0))
    if not last:
        grad = GradSteps(
            plan,
            tab,
            wh,
            wl,
            lambda n: [ebuf.at[n, a] for a in range(3)],
            gh,
            gl,
            dbuf,
            kbuf,
            True,
            outs,
            g_sem,
        )
    for s, (n, u) in enumerate(steps):
        if s == 0:
            wait_for(kbuf.at[0, pl.ds(3, 6)], k_sem.at[0])
        if u == 4 and n + 1 < chunks:
            wait_for(kbuf.at[n + 1], k_sem.at[n + 1])
            if n == 0 and not last:
                for other in range(chunks):
                    slope_copy(other).wait()
        if s == len(steps) - 2 and not last:
            for early in range(3):
                for copy in v_copies(early):
                    copy.start()
        tasks = []
        if s > 0:
            tasks += column_tasks(s - 1)
        if s + 1 < len(steps):
            next_n, next_u = steps[s + 1]
            if n == 0 and u < 4:
                tasks += cells(u + 1)
            tasks += tap_tasks(kbuf.at[next_n], uh.at[(s + 1) % 2], ul.at[(s + 1) % 2], next_u)
        if n > 0 and u > 0:
            tasks += part_of(finish_tasks(n - 1), u - 1, 4)
        if s + 1 == len(steps) and not last and chunks > 1:
            tasks += grad.cells(0)

        def put(v, value, s=s):
            mbuf[s % 2, v, pl.ds(1, T)] = value.reshape(T, R, N)

        interleave(
            dot_tasks(lambda v: (wh[u, v], wl[u, v]), lambda v: (uh[s % 2, v], ul[s % 2, v]), NT, put),
            tasks,
        )
    end = chunks - 1
    for n in range(end):
        out_copy(n).start()
    closing = column_tasks(len(steps) - 1) + finish_tasks(end)
    if last:
        run_all(closing)
        out_copy(end).start()
        for n in range(chunks):
            out_copy(n).wait()
        return

    for late in range(3, 5):
        for copy in v_copies(late):
            copy.start()
    if chunks == 1:
        run_all(closing)
        run_all(grad.cells(0))
    for early in range(3):
        for copy in v_copies(early):
            copy.wait()
    for s, (n, u) in enumerate(steps):
        if s == 2:
            for late in range(3, 5):
                for copy in v_copies(late):
                    copy.wait()
        if s + 1 == len(steps) - 3:
            out_copy(end).start()
            for done in range(end):
                grad.store(done)
            bias_rows[...] = jnp.broadcast_to(jnp.sum(total[...], axis=0, keepdims=True), (8, C))
            bias_sum[...] = bias_rows[0:1]
            for copy in bias_copies(plan, bias_rows, outs, bias_sem):
                copy.start()
        tasks = []
        if chunks > 1 and s < 4:
            tasks += part_of(closing, s, 4)
        if s > 0:
            tasks += grad.adds(s - 1)
        if s + 1 < len(steps):
            tasks += grad.cells(s + 1)
        interleave(grad.dots(s), tasks)
    run_all(grad.adds(len(steps) - 1))
    grad.store(end)
    for n in range(chunks):
        out_copy(n).wait()
    for copy in bias_copies(plan, bias_rows, outs, bias_sem):
        copy.wait()
    grad.wait()


SMEM_SPEC = pl.BlockSpec(memory_space=pltpu.SMEM)
VMEM_SPEC = pl.BlockSpec(memory_space=pltpu.VMEM)
ANY_SPEC = pl.BlockSpec(memory_space=pl.ANY)


def plane_shape(plan):
    return jax.ShapeDtypeStruct((3, 3 * plan.T, plan.R, plan.C), F32)


def point_scratch(plan, width):
    shape = (5, 5, plan.T, plan.R, width)
    return [pltpu.VMEM(shape, BF16), pltpu.VMEM(shape, BF16)]


def call(kernel, outs, in_specs, out_specs, scratch, flops, args, name):
    moved = sum(a.size * a.dtype.itemsize for a in args) + sum(o.size * 4 for o in outs)
    return pl.pallas_call(
        kernel,
        out_shape=outs,
        in_specs=in_specs,
        out_specs=out_specs,
        scratch_shapes=scratch,
        compiler_params=pltpu.CompilerParams(vmem_limit_bytes=VMEM_LIMIT),
        cost_estimate=pl.CostEstimate(flops=flops, bytes_accessed=moved, transcendentals=0),
        name=name,
    )(*args)


def pass_flops(plan):
    return 2 * 3 * 25 * plan.T * plan.R * plan.C * plan.C


def point_shape(plan):
    return jax.ShapeDtypeStruct((2, 5, 5, plan.T, plan.R, plan.C), BF16)


def grad_shapes(plan):
    blocks = 9 * plan.C // plan.block_rows // plan.n_outs
    block = plan.block_rows + (8 if plan.n_outs == 2 else 0)
    return [jax.ShapeDtypeStruct((blocks, block, plan.C), F32) for _ in range(plan.n_outs)]


def grad_scratch(plan):
    shape = (2, 5, plan.T, plan.R, plan.N)
    return [
        pltpu.VMEM((8, plan.C), F32),
        pltpu.VMEM(shape, BF16),
        pltpu.VMEM(shape, BF16),
        pltpu.VMEM((2, 5, plan.C, plan.N), F32),
    ]


def run_points(plan, x, name):
    scratch = [
        pltpu.VMEM((5, 3 * plan.T, plan.R, plan.C), F32),
        *point_scratch(plan, plan.C),
        pltpu.SemaphoreType.DMA((plan.C // LANES,)),
        pltpu.SemaphoreType.DMA((2, 5)),
    ]
    kernel = functools.partial(points_kernel, plan)
    return call(kernel, [point_shape(plan)], [ANY_SPEC], [ANY_SPEC], scratch, x.size * 40, [x], name)[0]


def run_forward(plan, tab, mask, bias, x, cot, pieces, name):
    last = cot is not None
    C, N, R, T = plan.C, plan.N, plan.R, plan.T
    cols = 3 * T
    chunks = C // N
    outs = [plane_shape(plan), plane_shape(plan)]
    scratch = [
        *point_scratch(plan, C),
        pltpu.VMEM((chunks, 9, C, N), F32),
        pltpu.VMEM((2, 5, C, N), BF16),
        pltpu.VMEM((2, 5, C, N), BF16),
        pltpu.VMEM((2, 5, T, R, N), F32),
        pltpu.VMEM((chunks, 5, cols, R, N), F32),
        pltpu.VMEM((chunks, cols, R, N), F32),
        pltpu.SemaphoreType.DMA((chunks + 1,)),
        pltpu.SemaphoreType.DMA((chunks, 3)),
    ]
    args = [tab, mask, bias, x]
    if last:
        outs += [jax.ShapeDtypeStruct((1, C), F32)] + grad_shapes(plan)
        out_specs = [ANY_SPEC, ANY_SPEC, VMEM_SPEC] + [ANY_SPEC] * plan.n_outs
        scratch += [
            pltpu.VMEM((5, cols, R, C), F32),
            pltpu.SemaphoreType.DMA((C // LANES,)),
            pltpu.VMEM((chunks, 3, cols, R, N), F32),
            pltpu.VMEM((16, C), F32),
            *grad_scratch(plan),
            pltpu.SemaphoreType.DMA((chunks,)),
            pltpu.SemaphoreType.DMA((chunks,)),
            pltpu.SemaphoreType.DMA,
        ]
        args.append(cot)
    else:
        out_specs = [ANY_SPEC] * 2
        scratch.append(pltpu.SemaphoreType.DMA((2, 5)))
    args += pieces
    in_specs = [SMEM_SPEC, VMEM_SPEC, VMEM_SPEC] + [ANY_SPEC] * (len(args) - 3)
    kernel = functools.partial(forward_kernel, plan, last, len(pieces))
    return call(kernel, outs, in_specs, out_specs, scratch, pass_flops(plan) * (1 + last), args, name)


def run_back(plan, tab, mask, y, slope, points, pieces, name):
    last = slope is None
    C, N, R, T = plan.C, plan.N, plan.R, plan.T
    cols = 3 * T
    chunks = C // N
    outs = [plane_shape(plan)]
    out_specs = [ANY_SPEC]
    scratch = [
        pltpu.VMEM((3, cols, R, C), F32),
        *point_scratch(plan, C),
        pltpu.VMEM((chunks, 9, N, C), F32),
        pltpu.VMEM((2, 5, N, C), BF16),
        pltpu.VMEM((2, 5, N, C), BF16),
        pltpu.VMEM((2, 5, T + 2, R, N), F32),
        pltpu.VMEM((chunks, 5, cols, R, N), F32),
        pltpu.SemaphoreType.DMA((C // LANES,)),
        pltpu.SemaphoreType.DMA((chunks + 1,)),
        pltpu.SemaphoreType.DMA((chunks,)),
    ]
    args = [tab, mask, y]
    if not last:
        outs += [jax.ShapeDtypeStruct((1, C), F32)] + grad_shapes(plan)
        out_specs += [VMEM_SPEC] + [ANY_SPEC] * plan.n_outs
        scratch += [
            pltpu.VMEM((chunks, 3, cols, R, N), F32),
            pltpu.VMEM((R, C), F32),
            *grad_scratch(plan),
            pltpu.SemaphoreType.DMA((chunks,)),
            pltpu.SemaphoreType.DMA((2, 5)),
            pltpu.SemaphoreType.DMA((chunks,)),
            pltpu.SemaphoreType.DMA,
        ]
        args += [slope, points]
    args += pieces
    mask_spec = VMEM_SPEC if last else ANY_SPEC
    in_specs = [SMEM_SPEC, mask_spec] + [ANY_SPEC] * (len(args) - 2)
    kernel = functools.partial(back_kernel, plan, last, len(pieces))
    return call(kernel, outs, in_specs, out_specs, scratch, pass_flops(plan) * (2 - last), args, name)


def to_planes(plan, cells):
    slots, side, _, channels = cells.shape
    tiled = cells.reshape(slots, plan.T, 3, side, channels).transpose(2, 3, 0, 1, 4)
    flat = tiled.reshape(3, side, slots * plan.T, channels)
    return jnp.pad(flat, ((0, 0), (0, 0), (0, plan.R - slots * plan.T), (0, 0)))


def from_planes(plan, planes, slots):
    side = 3 * plan.T
    kept = planes[:, :, : slots * plan.T].reshape(3, side, slots, plan.T, planes.shape[3])
    return kept.transpose(2, 3, 0, 1, 4).reshape(slots, side, side, planes.shape[3])


def tie(*values):
    return lax.optimization_barrier(values)


class Net:
    def __init__(self):
        self.rep = lax.axis_size("rep")
        self.dp = lax.axis_size("dp")
        self.routed = self.rep == 4 and self.dp == 8
        self.n_pieces = 4 if self.routed else 1
        self.n_outs = 2 if self.routed else 1

    def perm(self, move):
        pairs = []
        for x in range(2):
            for c in range(2):
                for z in range(4):
                    for y in range(2):
                        to = move(x, c, z, y)
                        pairs.append((((x * 2 + c) * 4 + z) * 2 + y, ((to[0] * 2 + to[1]) * 4 + to[2]) * 2 + to[3]))
        return pairs

    def send(self, value, move):
        return lax.ppermute(value, AXES, self.perm(move))

    def over_core(self, value):
        return self.send(value, lambda x, c, z, y: (x, 1 - c, z, y))

    def over_first(self, value):
        return self.send(value, lambda x, c, z, y: (x, c, z, 1 - y) if c == 0 else (1 - x, c, z, y))

    def over_second(self, value):
        return self.send(value, lambda x, c, z, y: (1 - x, c, z, y) if c == 0 else (x, c, z, 1 - y))

    def over_both(self, value):
        return self.send(value, lambda x, c, z, y: (1 - x, c, z, 1 - y))

    def over_z(self, value, step):
        return self.send(value, lambda x, c, z, y: (x, c, (z + step) % 4, y))

    def tables(self):
        if not self.routed:
            return jnp.zeros((4, 8), jnp.int32)
        rep = lax.axis_index("rep")
        dp = lax.axis_index("dp")
        x, c, z, y = rep // 2, rep % 2, dp // 2, dp % 2
        block = jnp.arange(32, dtype=jnp.int32)
        bx, bc, bz, by = block // 16, block // 8 % 2, block // 2 % 4, block % 2
        dx, dy = bx ^ x, by ^ y
        second = jnp.where(bc == 0, dx, dy)
        first = jnp.where(bc == 0, dy, dx)
        other = (bc != c).astype(jnp.int32)
        return jnp.stack(
            [2 * other + second, 4 * first + (z - bz) % 4, other, 8 * second + 4 * first + (bz - z) % 4]
        ).astype(jnp.int32)

    def gather_z(self, shard):
        return jnp.stack([shard] + [self.over_z(shard, step) for step in (1, 2, 3)])

    def double(self, part):
        return jnp.concatenate([part, self.over_first(part)])

    def gather_whole(self, shard):
        return [lax.all_gather(shard, AXES, axis=0, tiled=True)[None]]

    def sum_whole(self, parts):
        return lax.psum_scatter(parts[0][0], AXES, scatter_dimension=0, tiled=True)

    def send_z(self, four):
        return [four[0]] + [self.over_z(four[step], step) for step in (1, 2, 3)]


def body(
    features, map_size, item_count, conv4_weight, conv4_bias, conv5_weight, conv5_bias, cotangent
):
    slots, side, _, channels = features.shape
    net = Net()
    tiles = side // 3
    rows = -(-slots * tiles // 16) * 16
    shard_rows = conv4_weight.shape[0] // channels
    block_rows = shard_rows if net.routed else 9 * channels
    plan = Plan(channels, rows, tiles, block_rows, net.n_pieces, net.n_outs)

    live = jnp.arange(slots, dtype=jnp.int32) < item_count[0]
    inside = jnp.arange(side, dtype=jnp.int32)[None, :] < map_size[:, None]
    valid = live[:, None, None] & inside[:, :, None] & inside[:, None, :]
    mask = to_planes(plan, jnp.broadcast_to(valid.astype(F32)[..., None], (slots, side, side, LANES)))
    source = to_planes(plan, features * valid.astype(F32)[..., None])
    cot = to_planes(plan, cotangent)
    tab = net.tables()

    shard4 = conv4_weight.reshape(shard_rows, channels)
    shard5 = conv5_weight.reshape(shard_rows, channels)
    if net.routed:
        four4 = net.gather_z(shard4)
        shard5, four4, source, mask, cot = tie(shard5, four4, source, mask, cot)
        four5 = net.gather_z(shard5)
        eight4 = net.double(four4)
        far4 = net.over_second(eight4)
        four5, far4, eight4 = tie(four5, far4, eight4)
        points4 = run_points(plan, source, "points4")
        pieces4 = [eight4, far4, net.over_core(eight4), net.over_core(far4)]
        eight5 = net.double(four5)
        eight5, points4 = tie(eight5, points4)
        far5 = net.over_second(eight5)
        near5 = net.over_core(eight5)
    else:
        pieces4 = net.gather_whole(shard4)
        pieces5 = net.gather_whole(shard5)
        points4 = run_points(plan, source, "points4")
    hidden, slope4 = run_forward(plan, tab, mask, conv4_bias[None], points4, None, pieces4, "conv4")
    if net.routed:
        far5, near5, hidden = tie(far5, near5, hidden)
        pieces5 = [eight5, far5, near5, net.over_core(far5)]
    out5, back5, bias5, *grad5 = run_forward(
        plan, tab, mask, conv5_bias[None], hidden, cot, pieces5, "conv5_grad5"
    )
    if net.routed:
        mine5, other5 = grad5
        core5 = net.over_core(other5)
        sends5 = [mine5[i : i + 4] + core5[i : i + 4] for i in (4, 8, 12)]
        *sends5, back5 = tie(*sends5, back5)
        got5 = [net.over_first(sends5[0]), net.over_second(sends5[1]), net.over_both(sends5[2])]
    back4, bias4, *grad4 = run_back(plan, tab, mask, back5, slope4, points4, pieces5, "back5_grad4")
    if net.routed:
        mine4, theirs4, *got5 = tie(*grad4, *got5)
        core4 = net.over_core(theirs4)
        four5 = mine5[:4] + core5[:4] + got5[0] + got5[1] + got5[2]
        send4, four5, back4 = tie(mine4[8:] + core4[8:], four5, back4)
        second4 = net.over_second(send4)
        got5 = net.send_z(four5)
    input_grad = run_back(plan, tab, mask, back4, None, None, pieces4, "back4")[0]
    if net.routed:
        second4, input_grad, *got5 = tie(second4, input_grad, *got5)
        first4 = net.over_first(mine4[4:8] + core4[4:8] + second4[4:])
        sum4 = sum(net.send_z(mine4[:4] + core4[:4] + second4[:4] + first4))
        sum5 = sum(got5)
        share4, total4 = sum4[:shard_rows], sum4[shard_rows]
        share5, total5 = sum5[:shard_rows], sum5[shard_rows]
    else:
        share5 = net.sum_whole(grad5)
        share4 = net.sum_whole(grad4)
        total4, total5 = lax.psum((bias4[0], bias5[0]), AXES)

    total_cells = slots * net.rep * net.dp * side * side
    scale = float(total_cells) ** (-0.5)
    return (
        from_planes(plan, out5, slots),
        from_planes(plan, input_grad, slots),
        (share4 * scale).reshape(-1),
        total4 * scale,
        (share5 * scale).reshape(-1),
        total5 * scale,
    )


def solution(mesh):
    placed = (
        P(AXES, None, None, None),
        P(AXES),
        P(AXES),
        P(AXES),
        P(),
        P(AXES),
        P(),
        P(AXES, None, None, None),
    )
    return jax.shard_map(
        body,
        mesh=mesh,
        in_specs=placed,
        out_specs=(
            P(AXES, None, None, None),
            P(AXES, None, None, None),
            P(AXES),
            P(),
            P(AXES),
            P(),
        ),
        check_vma=False,
    )
```
